32 devices in a mesh: head: 4 (over y, x), ctx: 8 (over z, core).
Axes of the slice: x: 2, y: 2, z: 4, core: 2. Of those that a mesh axis runs over, the one named last changes fastest.
Arguments:
- queries: bfloat16 [8, 160, 4096], P('ctx', 'head'), may hold values from -4.5 to 4.5
- key_rows: bfloat16 [8, 160, 512], P('ctx', 'head'), may hold values from -4.5 to 4.5
- value_rows: bfloat16 [8, 160, 512], P('ctx', 'head'), may hold values from -6 to 6
- stretch_order: int32 [32], replicated, may hold values from 0 to 31, each once
- out_weight: bfloat16 [4096, 4096], P('head'), may hold values from -0.09375 to 0.09375
Outputs:
- projected: bfloat16 [1280, 4096], P('ctx', 'head')
The draws below stay inside these ranges and needn't reach their ends.
Inputs may be any that keep to these rules, and one draw needn't show every extreme that they name: stretch_order is a permutation of 0 to 31.
All inputs are finite; a program needn't handle non-finite values.
Results may differ from the reference program's by a relative error of at most 0.013.
Values may be sent and summed in bfloat16 or wider, within the bound.
No kernel may reach another device: no remote copies, remote signals or barrier semaphores. Data moves between devices by JAX's collectives and lax.ppermute only.
A program may use at most 64 MiB of HBM per device.

```python
import math
import jax
import jax.numpy as jnp
from jax import lax

D_HEAD = 128
QH = 32
KVH = 4
DO = 4096
TOK_CTX = 160
NB = 32
N_HEAD = 4
N_CTX = 8


def draw_queries(key, part):
    rows = N_CTX * TOK_CTX
    result = jax.random.truncated_normal(jax.random.fold_in(key, 11), -4.5, 4.5, (rows, QH, D_HEAD), jnp.float32)
    return result.reshape(N_CTX, TOK_CTX, QH * D_HEAD).astype(jnp.bfloat16)


def draw_key_rows(key, part):
    rows = N_CTX * TOK_CTX
    result = jax.random.truncated_normal(jax.random.fold_in(key, 12), -4.5, 4.5, (rows, KVH, D_HEAD), jnp.float32)
    return result.reshape(N_CTX, TOK_CTX, KVH * D_HEAD).astype(jnp.bfloat16)


def steps_of(own_key, extent, shards, least, top_value):
    loudness, own = 1.0, jax.random.fold_in(own_key, 6)
    for position, shards_of in shards:
        draws = jnp.exp(jax.random.uniform(jax.random.fold_in(own, position), (shards_of,), jnp.float32, least / len(shards), top_value / len(shards)))
        loudness = loudness * jnp.repeat(draws, extent[position] // shards_of).reshape([-1 if axis == position else 1 for axis in range(len(extent))])
    return loudness


def bell_draw(stream_key, shape, scale, bound, split=(), kind=jnp.bfloat16):
    gain = steps_of(stream_key, shape, split, -0.22, 0.18) if split else 1.0
    entries = jax.random.normal(stream_key, shape, jnp.float32) * scale * gain
    return jnp.minimum(jnp.maximum(entries, -bound), bound).astype(kind)


def setup_inputs(seed: int = 0) -> dict:
    streams_of = jax.random.split(jax.random.key(seed), 6)
    queries = draw_queries(jax.random.fold_in(streams_of[5], 71), 0)
    key_rows = draw_key_rows(jax.random.fold_in(streams_of[5], 71), 0)
    value_rows = bell_draw(streams_of[2], (N_CTX, TOK_CTX, KVH * D_HEAD), 1.0, 6.0, ((0, 8), (1, 4)))
    stretch_order = jax.random.permutation(streams_of[3], NB).astype(jnp.int32)
    out_weight = bell_draw(streams_of[4], (QH * D_HEAD, DO), (QH * D_HEAD) ** -0.5, 0.09375, ((0, 4),))
    return dict(queries=queries, key_rows=key_rows, value_rows=value_rows, stretch_order=stretch_order, out_weight=out_weight)


def reference(queries, key_rows, value_rows, stretch_order, out_weight):
    span = TOK_CTX // N_HEAD
    total_rows = N_CTX * TOK_CTX
    groups = QH // KVH
    flat_q = queries.reshape(total_rows, KVH, groups, D_HEAD)
    flat_k = key_rows.reshape(total_rows, KVH, D_HEAD).astype(jnp.float32)
    flat_v = value_rows.reshape(total_rows, KVH, D_HEAD).astype(jnp.float32)
    rows_all = jnp.arange(total_rows, dtype=jnp.int32)
    positions = (stretch_order[rows_all // span] * span + rows_all % span).astype(jnp.int32)
    block_rows = math.gcd(256, total_rows)

    def one_block(index):
        start = (index * block_rows).astype(jnp.int32)
        query_block = lax.dynamic_slice_in_dim(flat_q, start, block_rows, 0).astype(jnp.float32)
        query_pos = lax.dynamic_slice_in_dim(positions, start, block_rows, 0)
        scores = jnp.einsum("tkgd,skd->kgts", query_block, flat_k) * (D_HEAD ** -0.5)
        visible = positions[None, :] <= query_pos[:, None]
        scores = jnp.where(visible, scores, -1.0e30)
        peak = jnp.max(scores, axis=3, keepdims=True)
        weights = jnp.where(visible, jnp.exp(scores - peak), 0.0)
        denom = jnp.sum(weights, axis=3)
        rounded = lax.optimization_barrier(weights.astype(jnp.bfloat16)).astype(jnp.float32)
        mixed = jnp.einsum("kgts,skd->kgtd", rounded, flat_v) / denom[..., None]
        return jnp.transpose(mixed, (2, 0, 1, 3)).reshape(block_rows, QH * D_HEAD).astype(jnp.bfloat16)

    attn = lax.map(one_block, jnp.arange(total_rows // block_rows, dtype=jnp.int32))
    attn = attn.reshape(total_rows, QH * D_HEAD)
    width = QH * D_HEAD // N_HEAD
    total = jnp.zeros((total_rows, DO), jnp.float32)
    for part_index in range(N_HEAD):
        cols = attn[:, part_index * width:(part_index + 1) * width]
        rows_w = out_weight[part_index * width:(part_index + 1) * width, :]
        partial_value = jnp.dot(cols, rows_w, preferred_element_type=jnp.float32).astype(jnp.bfloat16)
        total = total + partial_value.astype(jnp.float32)
    return total.astype(jnp.bfloat16)
```

```python
import functools
import math

import jax
import jax.numpy as jnp
from jax import lax
from jax.experimental import pallas as pl
from jax.experimental.pallas import tpu as pltpu
from jax.sharding import PartitionSpec as P

D_HEAD = 128
NEG_FILL = -1e30
EXP2_SCALE = D_HEAD ** (-0.5) * math.log2(math.e)
ORDER = (3, 1, 2, 0)


def swap(x, axis, flip, size):
    return lax.ppermute(x, axis, [(i, i ^ flip) for i in range(size)])


def lookup_positions(order, flat_rows, span):
    table = jnp.arange(order.shape[0], dtype=jnp.int32)
    hits = (flat_rows // span)[:, None] == table[None, :]
    return jnp.sum(jnp.where(hits, order[None, :], 0), axis=1) * span + flat_rows % span


def attend_kernel(span, heads, n_piece, n_chunk, *refs):
    qpos_ref, kpos_ref = refs[:2]
    q_refs = refs[2 : 2 + n_piece]
    kv_refs = refs[2 + n_piece : 2 + n_piece + n_chunk]
    weight_ref, attn_ref, part_ref, k_s, v_s, bias_s, a_s, w_s, sem = refs[2 + n_piece + n_chunk :]
    me = lax.axis_index("head")
    cols = part_ref.shape[1]
    start = pl.multiple_of((me ^ ORDER[0]) * cols, cols)
    fetch = pltpu.make_async_copy(weight_ref.at[:, pl.ds(start, cols)], w_s, sem)
    fetch.start()
    rows = kv_refs[0].shape[0]
    for i, ref in enumerate(kv_refs):
        k_s[i * rows : (i + 1) * rows, :] = ref[:, :D_HEAD]
        v_s[i * rows : (i + 1) * rows, :] = ref[:, D_HEAD:]
    bias_s[...] = jnp.where(kpos_ref[...] <= qpos_ref[...], 0.0, NEG_FILL)
    for piece in range(n_piece):
        q = q_refs[piece][...].astype(jnp.float32)
        q = jnp.concatenate([q[:, h * D_HEAD : (h + 1) * D_HEAD] for h in range(heads)], axis=0)
        scores = lax.dot_general(
            q.astype(jnp.bfloat16), k_s[...], (((1,), (1,)), ((), ())),
            preferred_element_type=jnp.float32,
        )
        n_keys = scores.shape[1]
        scores = scores.reshape(heads, span, n_keys) + bias_s[piece * span : (piece + 1) * span, :][None]
        peak = jnp.max(scores, axis=2, keepdims=True)
        weights = jnp.exp2((scores - peak) * EXP2_SCALE)
        denom = jnp.sum(weights, axis=2, keepdims=True)
        mixed = jnp.dot(
            weights.astype(jnp.bfloat16).reshape(heads * span, n_keys), v_s[...],
            preferred_element_type=jnp.float32,
        )
        mixed = mixed.reshape(heads, span, D_HEAD) / denom
        at = pl.multiple_of((me ^ piece) * span, span)
        for h in range(heads):
            a_s[pl.ds(at, span), h * D_HEAD : (h + 1) * D_HEAD] = mixed[h]
    attn = a_s[...].astype(jnp.bfloat16)
    attn_ref[...] = attn
    fetch.wait()
    part_ref[...] = jnp.dot(attn, w_s[...], preferred_element_type=jnp.float32).astype(jnp.bfloat16)


def attend(q_pieces, kv_chunks, qpos, kpos, weight):
    n_piece, n_chunk = len(q_pieces), len(kv_chunks)
    span, width = q_pieces[0].shape
    heads = width // D_HEAD
    seg = span * n_piece
    rows = kv_chunks[0].shape[0]
    n_keys = rows * n_chunk
    cols = weight.shape[1] // n_piece
    vmem = pl.BlockSpec(memory_space=pltpu.VMEM)
    return pl.pallas_call(
        functools.partial(attend_kernel, span, heads, n_piece, n_chunk),
        out_shape=(
            jax.ShapeDtypeStruct((seg, width), jnp.bfloat16),
            jax.ShapeDtypeStruct((seg, cols), jnp.bfloat16),
        ),
        in_specs=[vmem] * (2 + n_piece + n_chunk) + [pl.BlockSpec(memory_space=pl.ANY)],
        out_specs=(vmem, vmem),
        scratch_shapes=[
            pltpu.VMEM((n_keys, D_HEAD), jnp.bfloat16),
            pltpu.VMEM((n_keys, D_HEAD), jnp.bfloat16),
            pltpu.VMEM((seg, n_keys), jnp.float32),
            pltpu.VMEM((seg, width), jnp.float32),
            pltpu.VMEM((weight.shape[0], cols), jnp.bfloat16),
            pltpu.SemaphoreType.DMA(()),
        ],
        compiler_params=pltpu.CompilerParams(vmem_limit_bytes=40 * 1024 * 1024),
        cost_estimate=pl.CostEstimate(
            flops=4 * seg * width * n_keys + 2 * seg * width * cols,
            bytes_accessed=8 * 1024 * 1024,
            transcendentals=seg * heads * n_keys,
        ),
    )(qpos, kpos, *q_pieces, *kv_chunks, weight)


def fast_path(queries, key_rows, value_rows, stretch_order, out_weight, n_head, n_ctx):
    me = lax.axis_index("head")
    ctx = lax.axis_index("ctx")
    span = queries.shape[1]
    kv_w = key_rows.shape[2] // n_head
    q_w = queries.shape[2] // n_head

    def cut(x, k, width):
        return lax.dynamic_slice_in_dim(x[0], (me ^ k) * width, width, 1)

    kv_cut = [
        jnp.concatenate([cut(key_rows, k, kv_w), cut(value_rows, k, kv_w)], axis=1)
        for k in range(n_head)
    ]
    q_cut = [cut(queries, k, q_w) for k in range(n_head)]
    kv_in = [kv_cut[0]] + [swap(kv_cut[k], "head", k, n_head) for k in range(1, n_head)]
    q_in = [q_cut[0]] + [swap(q_cut[k], "head", k, n_head) for k in range(1, n_head)]
    own = jnp.concatenate(kv_in, axis=0)
    same_core = [own] + [swap(own, "ctx", 2 * dz, n_ctx) for dz in range(1, n_ctx // 2)]
    other_core = [swap(x, "ctx", 1, n_ctx) for x in same_core]
    chunks = same_core + other_core
    chunk_ctx = [ctx ^ (2 * dz) for dz in range(n_ctx // 2)]
    chunk_ctx = chunk_ctx + [c ^ 1 for c in chunk_ctx]
    offsets = jnp.arange(span, dtype=jnp.int32)

    def positions(ctx_ids):
        blocks = jnp.stack([c * n_head + (me ^ k) for c in ctx_ids for k in range(n_head)])
        table = jnp.arange(stretch_order.shape[0], dtype=jnp.int32)
        held = jnp.sum(jnp.where(blocks[:, None] == table[None, :], stretch_order[None, :], 0), axis=1)
        return (held[:, None] * span + offsets[None, :]).reshape(-1)

    qpos = positions([ctx])[:, None]
    kpos = positions(chunk_ctx)[None, :]
    attn, far = attend(q_in, chunks, qpos, kpos, out_weight)
    out_w = out_weight.shape[1] // n_head
    total = swap(far, "head", ORDER[0], n_head).astype(jnp.float32)
    for k in ORDER[1:]:
        w = lax.dynamic_slice_in_dim(out_weight, (me ^ k) * out_w, out_w, 1)
        part = jnp.dot(attn, w, preferred_element_type=jnp.float32).astype(jnp.bfloat16)
        if k:
            part = swap(part, "head", k, n_head)
        total = total + part.astype(jnp.float32)
    return total.astype(jnp.bfloat16)


def attend_block(state, query_heads, query_pos, key_block, value_block, key_pos):
    run_max, run_sum, run_acc = state
    scores = jnp.einsum(
        "tkgd,pkd->kgtp", query_heads, key_block, preferred_element_type=jnp.float32
    ) * D_HEAD ** (-0.5)
    visible = key_pos[None, :] <= query_pos[:, None]
    scores = jnp.where(visible, scores, NEG_FILL)
    new_max = jnp.maximum(run_max, jnp.max(scores, axis=3))
    weights = jnp.where(visible, jnp.exp(scores - new_max[..., None]), 0.0)
    factor = jnp.exp(run_max - new_max)
    new_sum = run_sum * factor + jnp.sum(weights, axis=3)
    product = jnp.einsum(
        "kgtp,pkd->kgtd",
        weights.astype(jnp.bfloat16),
        value_block,
        preferred_element_type=jnp.float32,
    )
    return (new_max, new_sum, run_acc * factor[..., None] + product)


def fold_piece(
    state, query_heads, query_pos, key_piece, value_piece, flat_rows, order, span, kv_heads
):
    count = key_piece.shape[0]
    width = 512 if count % 512 == 0 else count
    blocks_n = count // width
    key_blocks = key_piece.reshape(blocks_n, width, kv_heads, D_HEAD)
    value_blocks = value_piece.reshape(blocks_n, width, kv_heads, D_HEAD)
    flat_blocks = flat_rows.reshape(blocks_n, width)

    def step_block(current, slab):
        key_block, value_block, block_rows = slab
        key_pos = lookup_positions(order, block_rows, span)
        return (
            attend_block(current, query_heads, query_pos, key_block, value_block, key_pos),
            None,
        )

    state, unused = lax.scan(step_block, state, (key_blocks, value_blocks, flat_blocks))
    return state


def long_path(queries, key_rows, value_rows, stretch_order, out_weight, n_head):
    ctx_index = lax.axis_index("ctx")
    span = queries.shape[1]
    seg_rows = span * n_head
    kv_local = key_rows.shape[2] // D_HEAD // n_head
    q_local = queries.shape[2] // D_HEAD // n_head
    groups = q_local // kv_local
    query_flat = ctx_index * seg_rows + jnp.arange(seg_rows, dtype=jnp.int32)
    query_pos = lookup_positions(stretch_order, query_flat, span)
    initial = (
        jnp.full((kv_local, groups, seg_rows), NEG_FILL, jnp.float32),
        jnp.zeros((kv_local, groups, seg_rows), jnp.float32),
        jnp.zeros((kv_local, groups, seg_rows, D_HEAD), jnp.float32),
    )
    query_ex, key_ex, value_ex = (
        lax.all_to_all(queries, "head", split_axis=2, concat_axis=1, tiled=True),
        lax.all_to_all(key_rows, "head", split_axis=2, concat_axis=1, tiled=True),
        lax.all_to_all(value_rows, "head", split_axis=2, concat_axis=1, tiled=True),
    )
    query_heads = query_ex[0].reshape(seg_rows, kv_local, groups, D_HEAD)
    keys = lax.all_gather(key_ex[0], "ctx", axis=0, tiled=True)
    values = lax.all_gather(value_ex[0], "ctx", axis=0, tiled=True)
    flat_rows = jnp.arange(keys.shape[0], dtype=jnp.int32)
    final = fold_piece(
        initial, query_heads, query_pos, keys, values, flat_rows, stretch_order, span, kv_local
    )
    run_max, run_sum, run_acc = final
    mixed = run_acc / run_sum[..., None]
    attn = (
        jnp.transpose(mixed, (2, 0, 1, 3)).reshape(seg_rows, q_local * D_HEAD).astype(jnp.bfloat16)
    )
    partial_out = jnp.dot(attn, out_weight, preferred_element_type=jnp.float32).astype(jnp.bfloat16)
    return (
        lax.psum_scatter(partial_out, "head", scatter_dimension=1, tiled=True)
        .astype(jnp.float32)
        .astype(jnp.bfloat16)
    )


def solution(mesh):
    n_head, n_ctx = mesh.shape["head"], mesh.shape["ctx"]

    def on_device(*args):
        if n_ctx <= 8:
            return fast_path(*args, n_head, n_ctx)
        return long_path(*args, n_head)

    return jax.shard_map(
        on_device,
        mesh=mesh,
        in_specs=(
            P("ctx", "head", None),
            P("ctx", "head", None),
            P("ctx", "head", None),
            P(),
            P("head", None),
        ),
        out_specs=P("ctx", "head"),
        check_vma=False,
    )
```

```python
import functools
import math

import jax
import jax.numpy as jnp
from jax import lax
from jax.experimental import pallas as pl
from jax.experimental.pallas import tpu as pltpu
from jax.sharding import PartitionSpec as P

D_HEAD = 128
NEG_FILL = -1e30
ROOMY = 42
FETCHES = 8
EXP2_SCALE = D_HEAD ** (-0.5) * math.log2(math.e)


def swap(x, axis, flip, size):
    return lax.ppermute(x, axis, [(i, i ^ flip) for i in range(size)])


def lookup_positions(order, flat_rows, span):
    table = jnp.arange(order.shape[0], dtype=jnp.int32)
    hits = (flat_rows // span)[:, None] == table[None, :]
    return jnp.sum(jnp.where(hits, order[None, :], 0), axis=1) * span + flat_rows % span


def stack_heads(q_ref, heads):
    q = q_ref[...].astype(jnp.float32)
    q = jnp.concatenate([q[:, h * D_HEAD : (h + 1) * D_HEAD] for h in range(heads)], axis=0)
    return q.astype(jnp.bfloat16)


def prepare_kernel(span, n_head, chunk_flips, order_ref, weight_ref, after_ref, *refs):
    q_refs, (weight_out, bias_ref, q_out, sems) = refs[:n_head], refs[n_head:]
    me, ctx = lax.axis_index("head"), lax.axis_index("ctx")
    step = weight_ref.shape[0] // FETCHES
    fetches = [
        pltpu.make_async_copy(
            weight_ref.at[i * step : (i + 1) * step], weight_out.at[i * step : (i + 1) * step], sems.at[i]
        )
        for i in range(FETCHES)
    ]

    @pl.when(me >= 0)
    def start():
        for fetch in fetches:
            fetch.start()

    n_keys = bias_ref.shape[1]
    lane = lax.broadcasted_iota(jnp.int32, (1, n_keys), 1)
    kpos = lane
    for i, flip in enumerate(chunk_flips):
        for k in range(n_head):
            first = (i * n_head + k) * span
            block = order_ref[(ctx ^ flip) * n_head + (me ^ k)]
            kpos = jnp.where(lane >= first, lane + (block * span - first), kpos)
    row = lax.broadcasted_iota(jnp.int32, (span, 1), 0)
    for k in range(n_head):
        qpos = row + order_ref[ctx * n_head + (me ^ k)] * span
        bias_ref[k * span : (k + 1) * span, :] = jnp.where(kpos <= qpos, 0.0, NEG_FILL)
        q_out[k] = stack_heads(q_refs[k], q_refs[k].shape[1] // D_HEAD)
    for fetch in fetches:
        fetch.wait()


def prepare(order, weight, after, q_pieces, chunk_flips, n_keys):
    n_head = len(q_pieces)
    span, width = q_pieces[0].shape
    vmem = pl.BlockSpec(memory_space=pltpu.VMEM)
    return pl.pallas_call(
        functools.partial(prepare_kernel, span, n_head, chunk_flips),
        out_shape=(
            jax.ShapeDtypeStruct(weight.shape, weight.dtype),
            jax.ShapeDtypeStruct((span * n_head, n_keys), jnp.float32),
            jax.ShapeDtypeStruct((n_head, span * width // D_HEAD, D_HEAD), jnp.bfloat16),
        ),
        in_specs=[
            pl.BlockSpec(memory_space=pltpu.SMEM),
            pl.BlockSpec(memory_space=pltpu.HBM),
            pl.BlockSpec(memory_space=pl.ANY),
        ]
        + [vmem] * n_head,
        out_specs=(vmem,) * 3,
        scratch_shapes=[pltpu.SemaphoreType.DMA((FETCHES,))],
        compiler_params=pltpu.CompilerParams(vmem_limit_bytes=ROOMY * 1024 * 1024),
        cost_estimate=pl.CostEstimate(flops=0, bytes_accessed=4 * 1024 * 1024, transcendentals=0),
    )(order, weight, after, *q_pieces)


def project(attn, weight_ref, me, flip, cols):
    at = pl.multiple_of((me ^ flip) * cols, cols)
    part = jnp.dot(attn, weight_ref[:, pl.ds(at, cols)], preferred_element_type=jnp.float32)
    return part.astype(jnp.bfloat16)


def gather_keys(kv_refs, k_s, v_s):
    rows = kv_refs[0].shape[0]
    for i, ref in enumerate(kv_refs):
        k_s[i * rows : (i + 1) * rows, :] = ref[:, :D_HEAD]
        v_s[i * rows : (i + 1) * rows, :] = ref[:, D_HEAD:]


def masked_scores(q, k_s, bias):
    scores = lax.dot_general(
        q, k_s[...], (((1,), (1,)), ((), ())), preferred_element_type=jnp.float32
    )
    span, n_keys = bias.shape
    return scores.reshape(-1, span, n_keys) + bias[None]


def mix_values(weights, v_s):
    heads, span, n_keys = weights.shape
    mixed = jnp.dot(
        weights.reshape(heads * span, n_keys), v_s[...], preferred_element_type=jnp.float32
    )
    return mixed.reshape(heads, span, D_HEAD)


def staged(n_piece, score, weigh, finish):
    scores, held = score(0), None
    for piece in range(n_piece):
        ahead = score(piece + 1) if piece + 1 < n_piece else None
        weights = weigh(piece, scores)
        if held is not None:
            finish(piece - 1, *held)
        scores, held = ahead, weights
    finish(n_piece - 1, *held)


def early_kernel(span, n_piece, n_chunk, *refs):
    bias_ref, q_ref = refs[:2]
    kv_refs = refs[2 : 2 + n_chunk]
    peak_ref, denom_ref, mixed_ref, k_s, v_s = refs[2 + n_chunk :]
    gather_keys(kv_refs, k_s, v_s)
    n_keys = k_s.shape[0]

    def score(piece):
        return masked_scores(q_ref[piece], k_s, bias_ref[piece * span : (piece + 1) * span, :n_keys])

    def weigh(piece, scores):
        peak = jnp.max(scores, axis=2, keepdims=True)
        weights = jnp.exp2((scores - peak) * EXP2_SCALE)
        peak_ref[piece] = peak
        denom_ref[piece] = jnp.sum(weights, axis=2, keepdims=True)
        return (weights.astype(jnp.bfloat16),)

    def finish(piece, weights):
        mixed_ref[piece] = mix_values(weights, v_s)

    staged(n_piece, score, weigh, finish)


def early_attend(bias, q_all, kv_chunks):
    n_chunk, (n_piece, stacked, depth) = len(kv_chunks), q_all.shape
    span = bias.shape[0] // n_piece
    heads = stacked // span
    n_keys = kv_chunks[0].shape[0] * n_chunk
    vmem = pl.BlockSpec(memory_space=pltpu.VMEM)
    column = jax.ShapeDtypeStruct((n_piece, heads, span, 1), jnp.float32)
    return pl.pallas_call(
        functools.partial(early_kernel, span, n_piece, n_chunk),
        out_shape=(column, column, jax.ShapeDtypeStruct((n_piece, heads, span, depth), jnp.float32)),
        in_specs=[vmem] * (2 + n_chunk),
        out_specs=(vmem,) * 3,
        scratch_shapes=[pltpu.VMEM((n_keys, D_HEAD), jnp.bfloat16)] * 2,
        compiler_params=pltpu.CompilerParams(vmem_limit_bytes=20 * 1024 * 1024),
        cost_estimate=pl.CostEstimate(
            flops=4 * n_piece * stacked * depth * n_keys,
            bytes_accessed=4 * 1024 * 1024,
            transcendentals=n_piece * stacked * n_keys,
        ),
    )(bias, q_all, *kv_chunks)


def attend_kernel(span, n_piece, n_chunk, *refs):
    bias_ref, q_ref = refs[:2]
    kv_refs = refs[2 : 2 + n_chunk]
    rest = refs[2 + n_chunk :]
    peak_ref, denom_ref, mixed_ref, weight_ref, attn_ref, low_ref, high_ref = rest[:7]
    k_s, v_s, a_s = rest[7:]
    me = lax.axis_index("head")
    gather_keys(kv_refs, k_s, v_s)
    n_keys = k_s.shape[0]

    def score(piece):
        return masked_scores(q_ref[piece], k_s, bias_ref[piece * span : (piece + 1) * span, n_keys:])

    def weigh(piece, scores):
        peak = jnp.maximum(peak_ref[piece], jnp.max(scores, axis=2, keepdims=True))
        weights = jnp.exp2((scores - peak) * EXP2_SCALE)
        factor = jnp.exp2((peak_ref[piece] - peak) * EXP2_SCALE)
        denom = factor * denom_ref[piece] + jnp.sum(weights, axis=2, keepdims=True)
        return weights.astype(jnp.bfloat16), factor, denom

    def finish(piece, weights, factor, denom):
        mixed = (factor * mixed_ref[piece] + mix_values(weights, v_s)) / denom
        at = pl.multiple_of((me ^ piece) * span, span)
        for h in range(mixed.shape[0]):
            a_s[pl.ds(at, span), h * D_HEAD : (h + 1) * D_HEAD] = mixed[h]

    staged(n_piece, score, weigh, finish)
    attn = a_s[...].astype(jnp.bfloat16)
    attn_ref[...] = attn
    part = project(attn, weight_ref, me, 3, low_ref.shape[1])
    half = low_ref.shape[0]
    low_ref[...] = part[:half]
    high_ref[...] = part[half:]


def attend(bias, kv_chunks, state, weight):
    n_chunk = len(kv_chunks)
    n_piece, heads, span, depth = state[-1].shape
    width = heads * depth
    seg = span * n_piece
    n_keys = kv_chunks[0].shape[0] * n_chunk
    cols = weight.shape[1] // n_piece
    vmem = pl.BlockSpec(memory_space=pltpu.VMEM)
    half = jax.ShapeDtypeStruct((seg // 2, cols), jnp.bfloat16)
    return pl.pallas_call(
        functools.partial(attend_kernel, span, n_piece, n_chunk),
        out_shape=(jax.ShapeDtypeStruct((seg, width), jnp.bfloat16), half, half),
        in_specs=[vmem] * (6 + n_chunk),
        out_specs=(vmem, vmem, vmem),
        scratch_shapes=[
            pltpu.VMEM((n_keys, D_HEAD), jnp.bfloat16),
            pltpu.VMEM((n_keys, D_HEAD), jnp.bfloat16),
            pltpu.VMEM((seg, width), jnp.float32),
        ],
        compiler_params=pltpu.CompilerParams(vmem_limit_bytes=28 * 1024 * 1024),
        cost_estimate=pl.CostEstimate(
            flops=4 * seg * width * n_keys + 2 * seg * width * cols,
            bytes_accessed=4 * 1024 * 1024,
            transcendentals=seg * heads * n_keys,
        ),
    )(bias, state[0], *kv_chunks, *state[1:], weight)


def project_kernel(flips, attn_ref, weight_ref, *out_refs):
    me = lax.axis_index("head")
    half, cols = out_refs[0].shape
    for i, flip in enumerate(flips):
        part = project(attn_ref[...], weight_ref, me, flip, cols)
        out_refs[2 * i][...] = part[:half]
        out_refs[2 * i + 1][...] = part[half:]


def project_rest(attn, weight, flips, n_head):
    seg, width = attn.shape
    n, cols = len(flips), weight.shape[1] // n_head
    vmem = pl.BlockSpec(memory_space=pltpu.VMEM)
    half = jax.ShapeDtypeStruct((seg // 2, cols), jnp.bfloat16)
    return pl.pallas_call(
        functools.partial(project_kernel, flips),
        out_shape=(half,) * (2 * n),
        in_specs=[vmem, vmem],
        out_specs=(vmem,) * (2 * n),
        compiler_params=pltpu.CompilerParams(vmem_limit_bytes=20 * 1024 * 1024),
        cost_estimate=pl.CostEstimate(
            flops=2 * seg * width * cols * n,
            bytes_accessed=2 * width * cols * n,
            transcendentals=0,
        ),
    )(attn, weight)


def add_kernel(a_ref, b_ref, out_ref):
    out_ref[...] = (a_ref[...].astype(jnp.float32) + b_ref[...].astype(jnp.float32)).astype(jnp.bfloat16)


def add_pair(a, b):
    vmem = pl.BlockSpec(memory_space=pltpu.VMEM)
    return pl.pallas_call(
        add_kernel,
        out_shape=jax.ShapeDtypeStruct(a.shape, jnp.bfloat16),
        in_specs=[vmem, vmem],
        out_specs=vmem,
        compiler_params=pltpu.CompilerParams(vmem_limit_bytes=6 * 1024 * 1024),
        cost_estimate=pl.CostEstimate(flops=a.size, bytes_accessed=6 * a.size, transcendentals=0),
    )(a, b)


def final_kernel(*refs):
    out_ref = refs[-1]
    half = out_ref.shape[0] // 2
    for i in range(2):
        total = sum(ref[...].astype(jnp.float32) for ref in refs[3 * i : 3 * i + 3])
        out_ref[i * half : (i + 1) * half, :] = total.astype(jnp.bfloat16)


def final_sum(low, high):
    vmem = pl.BlockSpec(memory_space=pltpu.VMEM)
    rows, cols = low[0].shape
    return pl.pallas_call(
        final_kernel,
        out_shape=jax.ShapeDtypeStruct((2 * rows, cols), jnp.bfloat16),
        in_specs=[vmem] * 6,
        out_specs=vmem,
        compiler_params=pltpu.CompilerParams(vmem_limit_bytes=6 * 1024 * 1024),
        cost_estimate=pl.CostEstimate(flops=4 * rows * cols, bytes_accessed=16 * rows * cols, transcendentals=0),
    )(*low, *high)


def fast_path(queries, key_rows, value_rows, stretch_order, out_weight, n_head, n_ctx):
    me = lax.axis_index("head")

    def cut(x, k):
        width = x.shape[2] // n_head
        return lax.dynamic_slice_in_dim(x[0], (me ^ k) * width, width, 1)

    kv_cut = [
        jnp.concatenate([cut(key_rows, k), cut(value_rows, k)], axis=1) for k in range(n_head)
    ]
    q_cut = [cut(queries, k) for k in range(n_head)]
    kv_in = [kv_cut[0]] + [swap(kv_cut[k], "head", k, n_head) for k in range(1, n_head)]
    own = jnp.concatenate(kv_in, axis=0)
    q_in = [q_cut[0]] + [swap(q_cut[k], "head", k, n_head) for k in range(1, n_head)]
    flips = [2 * dz for dz in range(n_ctx // 2)]
    chunk_flips = tuple(flips + [f ^ 1 for f in flips])
    weight, bias, q_all = prepare(stretch_order, out_weight, own, q_in, chunk_flips, own.shape[0] * n_ctx)
    far_keys = [swap(own, "ctx", f, n_ctx) for f in flips[1:]]
    far_keys, bias = lax.optimization_barrier((far_keys, bias))
    same_core = [own] + far_keys
    other_core = [swap(x, "ctx", 1, n_ctx) for x in same_core]
    state = early_attend(bias, q_all, same_core)
    attn, far_low, far_high = attend(bias, other_core, (q_all, *state), weight)
    x_far = swap(far_low, "head", 1, n_head)
    y_far = swap(far_high, "head", 2, n_head)
    x_low, x_high, y_low, y_high = project_rest(attn, weight, (1, 2), n_head)
    x_near = swap(x_low, "head", 1, n_head)
    y_near = swap(y_high, "head", 2, n_head)
    own_low, own_high = project_rest(attn, weight, (0,), n_head)
    y_sum = swap(add_pair(y_low, x_far), "head", 2, n_head)
    x_sum = swap(add_pair(x_high, y_far), "head", 1, n_head)
    return final_sum((own_low, x_near, y_sum), (own_high, y_near, x_sum))


def attend_block(state, query_heads, query_pos, key_block, value_block, key_pos):
    run_max, run_sum, run_acc = state
    scores = jnp.einsum(
        "tkgd,pkd->kgtp", query_heads, key_block, preferred_element_type=jnp.float32
    ) * D_HEAD ** (-0.5)
    visible = key_pos[None, :] <= query_pos[:, None]
    scores = jnp.where(visible, scores, NEG_FILL)
    new_max = jnp.maximum(run_max, jnp.max(scores, axis=3))
    weights = jnp.where(visible, jnp.exp(scores - new_max[..., None]), 0.0)
    factor = jnp.exp(run_max - new_max)
    new_sum = run_sum * factor + jnp.sum(weights, axis=3)
    product = jnp.einsum(
        "kgtp,pkd->kgtd",
        weights.astype(jnp.bfloat16),
        value_block,
        preferred_element_type=jnp.float32,
    )
    return (new_max, new_sum, run_acc * factor[..., None] + product)


def fold_piece(
    state, query_heads, query_pos, key_piece, value_piece, flat_rows, order, span, kv_heads
):
    count = key_piece.shape[0]
    width = 512 if count % 512 == 0 else count
    blocks_n = count // width
    key_blocks = key_piece.reshape(blocks_n, width, kv_heads, D_HEAD)
    value_blocks = value_piece.reshape(blocks_n, width, kv_heads, D_HEAD)
    flat_blocks = flat_rows.reshape(blocks_n, width)

    def step_block(current, slab):
        key_block, value_block, block_rows = slab
        key_pos = lookup_positions(order, block_rows, span)
        return (
            attend_block(current, query_heads, query_pos, key_block, value_block, key_pos),
            None,
        )

    state, unused = lax.scan(step_block, state, (key_blocks, value_blocks, flat_blocks))
    return state


def long_path(queries, key_rows, value_rows, stretch_order, out_weight, n_head):
    ctx_index = lax.axis_index("ctx")
    span = queries.shape[1]
    seg_rows = span * n_head
    kv_local = key_rows.shape[2] // D_HEAD // n_head
    q_local = queries.shape[2] // D_HEAD // n_head
    groups = q_local // kv_local
    query_flat = ctx_index * seg_rows + jnp.arange(seg_rows, dtype=jnp.int32)
    query_pos = lookup_positions(stretch_order, query_flat, span)
    initial = (
        jnp.full((kv_local, groups, seg_rows), NEG_FILL, jnp.float32),
        jnp.zeros((kv_local, groups, seg_rows), jnp.float32),
        jnp.zeros((kv_local, groups, seg_rows, D_HEAD), jnp.float32),
    )
    query_ex, key_ex, value_ex = (
        lax.all_to_all(queries, "head", split_axis=2, concat_axis=1, tiled=True),
        lax.all_to_all(key_rows, "head", split_axis=2, concat_axis=1, tiled=True),
        lax.all_to_all(value_rows, "head", split_axis=2, concat_axis=1, tiled=True),
    )
    query_heads = query_ex[0].reshape(seg_rows, kv_local, groups, D_HEAD)
    keys = lax.all_gather(key_ex[0], "ctx", axis=0, tiled=True)
    values = lax.all_gather(value_ex[0], "ctx", axis=0, tiled=True)
    flat_rows = jnp.arange(keys.shape[0], dtype=jnp.int32)
    final = fold_piece(
        initial, query_heads, query_pos, keys, values, flat_rows, stretch_order, span, kv_local
    )
    run_max, run_sum, run_acc = final
    mixed = run_acc / run_sum[..., None]
    attn = (
        jnp.transpose(mixed, (2, 0, 1, 3)).reshape(seg_rows, q_local * D_HEAD).astype(jnp.bfloat16)
    )
    partial_out = jnp.dot(attn, out_weight, preferred_element_type=jnp.float32).astype(jnp.bfloat16)
    return (
        lax.psum_scatter(partial_out, "head", scatter_dimension=1, tiled=True)
        .astype(jnp.float32)
        .astype(jnp.bfloat16)
    )


def solution(mesh):
    n_head, n_ctx = mesh.shape["head"], mesh.shape["ctx"]

    def on_device(*args):
        if n_ctx <= 8:
            return fast_path(*args, n_head, n_ctx)
        return long_path(*args, n_head)

    return jax.shard_map(
        on_device,
        mesh=mesh,
        in_specs=(
            P("ctx", "head", None),
            P("ctx", "head", None),
            P("ctx", "head", None),
            P(),
            P("head", None),
        ),
        out_specs=P("ctx", "head"),
        check_vma=False,
    )
```

```python
import functools
import math

import jax
import jax.numpy as jnp
from jax import lax
from jax.experimental import pallas as pl
from jax.experimental.pallas import tpu as pltpu
from jax.sharding import PartitionSpec as P

D_HEAD = 128
NEG_FILL = -1e30
ROOMY = 42
FETCHES = 8
EXP2_SCALE = D_HEAD ** (-0.5) * math.log2(math.e)


def swap(x, axis, flip, size):
    return lax.ppermute(x, axis, [(i, i ^ flip) for i in range(size)])


def lookup_positions(order, flat_rows, span):
    table = jnp.arange(order.shape[0], dtype=jnp.int32)
    hits = (flat_rows // span)[:, None] == table[None, :]
    return jnp.sum(jnp.where(hits, order[None, :], 0), axis=1) * span + flat_rows % span


def prepare_kernel(span, n_head, chunk_flips, order_ref, weight_ref, after_ref, *refs):
    q_refs, (weight_out, qpos_ref, kpos_ref, q_out, q_s, sems) = refs[:n_head], refs[n_head:]
    me, ctx = lax.axis_index("head"), lax.axis_index("ctx")
    step = weight_ref.shape[0] // FETCHES
    fetches = [
        pltpu.make_async_copy(
            weight_ref.at[i * step : (i + 1) * step], weight_out.at[i * step : (i + 1) * step], sems.at[i]
        )
        for i in range(FETCHES)
    ]

    @pl.when(me >= 0)
    def start():
        for fetch in fetches:
            fetch.start()

    row = lax.broadcasted_iota(jnp.int32, (span, D_HEAD), 0)
    for i, flip in enumerate(chunk_flips):
        for k in range(n_head):
            first = (i * n_head + k) * span
            block = order_ref[(ctx ^ flip) * n_head + (me ^ k)]
            kpos_ref[first : first + span, :] = row + block * span
    heads = q_refs[0].shape[1] // D_HEAD
    lane = lax.broadcasted_iota(jnp.int32, qpos_ref.shape, 1)
    qpos = lane
    for i in range(heads * n_head):
        block = order_ref[ctx * n_head + i % n_head]
        qpos = jnp.where(lane >= i * span, lane + (block - i) * span, qpos)
    qpos_ref[...] = qpos
    for k in range(n_head):
        at = pl.multiple_of((me ^ k) * span, span)
        q_s[pl.ds(at, span), :] = q_refs[k][...].astype(jnp.float32)
    stacked = jnp.concatenate([q_s[:, h * D_HEAD : (h + 1) * D_HEAD] for h in range(heads)], axis=0)
    q_out[...] = stacked.T.astype(jnp.bfloat16)
    for fetch in fetches:
        fetch.wait()


def prepare(order, weight, after, q_pieces, chunk_flips, n_keys):
    n_head = len(q_pieces)
    span, width = q_pieces[0].shape
    columns = span * n_head * width // D_HEAD
    vmem = pl.BlockSpec(memory_space=pltpu.VMEM)
    return pl.pallas_call(
        functools.partial(prepare_kernel, span, n_head, chunk_flips),
        out_shape=(
            jax.ShapeDtypeStruct(weight.shape, weight.dtype),
            jax.ShapeDtypeStruct((1, columns), jnp.int32),
            jax.ShapeDtypeStruct((n_keys, D_HEAD), jnp.int32),
            jax.ShapeDtypeStruct((D_HEAD, columns), jnp.bfloat16),
        ),
        in_specs=[
            pl.BlockSpec(memory_space=pltpu.SMEM),
            pl.BlockSpec(memory_space=pltpu.HBM),
            pl.BlockSpec(memory_space=pl.ANY),
        ]
        + [vmem] * n_head,
        out_specs=(vmem,) * 4,
        scratch_shapes=[
            pltpu.VMEM((span * n_head, width), jnp.float32),
            pltpu.SemaphoreType.DMA((FETCHES,)),
        ],
        compiler_params=pltpu.CompilerParams(vmem_limit_bytes=ROOMY * 1024 * 1024),
        cost_estimate=pl.CostEstimate(flops=0, bytes_accessed=4 * 1024 * 1024, transcendentals=0),
    )(order, weight, after, *q_pieces)


def project(attn, weight_ref, me, flip, cols):
    at = pl.multiple_of((me ^ flip) * cols, cols)
    part = jnp.dot(attn, weight_ref[:, pl.ds(at, cols)], preferred_element_type=jnp.float32)
    return part.astype(jnp.bfloat16)


def masked_scores(kv_refs, kpos, qpos_ref, q_ref):
    keys = jnp.concatenate([ref[:, :D_HEAD] for ref in kv_refs], axis=0)
    scores = jnp.dot(keys, q_ref[...], preferred_element_type=jnp.float32)
    kpos = jnp.concatenate([kpos] * (scores.shape[1] // D_HEAD), axis=1)
    return jnp.where(kpos <= qpos_ref[...], scores, NEG_FILL)


def mix_values(kv_refs, weights):
    values = jnp.concatenate([ref[:, D_HEAD:] for ref in kv_refs], axis=0)
    return jnp.dot(values.T, weights.astype(jnp.bfloat16), preferred_element_type=jnp.float32)


def early_kernel(n_chunk, kpos_ref, qpos_ref, q_ref, *refs):
    kv_refs, (peak_ref, denom_ref, mixed_ref) = refs[:n_chunk], refs[n_chunk:]
    n_keys = kv_refs[0].shape[0] * n_chunk
    scores = masked_scores(kv_refs, kpos_ref[:n_keys, :], qpos_ref, q_ref)
    peak = jnp.max(scores, axis=0, keepdims=True)
    weights = jnp.exp2((scores - peak) * EXP2_SCALE)
    peak_ref[...] = peak
    denom_ref[...] = jnp.sum(weights, axis=0, keepdims=True)
    mixed_ref[...] = mix_values(kv_refs, weights)


def early_attend(kpos, qpos, q_all, kv_chunks):
    n_chunk, (depth, columns) = len(kv_chunks), q_all.shape
    n_keys = kv_chunks[0].shape[0] * n_chunk
    vmem = pl.BlockSpec(memory_space=pltpu.VMEM)
    line = jax.ShapeDtypeStruct((1, columns), jnp.float32)
    return pl.pallas_call(
        functools.partial(early_kernel, n_chunk),
        out_shape=(line, line, jax.ShapeDtypeStruct((depth, columns), jnp.float32)),
        in_specs=[vmem] * (3 + n_chunk),
        out_specs=(vmem,) * 3,
        compiler_params=pltpu.CompilerParams(vmem_limit_bytes=20 * 1024 * 1024),
        cost_estimate=pl.CostEstimate(
            flops=4 * columns * depth * n_keys,
            bytes_accessed=4 * 1024 * 1024,
            transcendentals=columns * n_keys,
        ),
    )(kpos, qpos, q_all, *kv_chunks)


def attend_kernel(n_chunk, kpos_ref, qpos_ref, q_ref, *refs):
    kv_refs = refs[:n_chunk]
    peak_ref, denom_ref, mixed_ref, weight_ref, attn_ref, low_ref, high_ref = refs[n_chunk:]
    seg, width = attn_ref.shape
    n_keys = kv_refs[0].shape[0] * n_chunk
    scores = masked_scores(kv_refs, kpos_ref[n_keys:, :], qpos_ref, q_ref)
    peak = jnp.maximum(peak_ref[...], jnp.max(scores, axis=0, keepdims=True))
    weights = jnp.exp2((scores - peak) * EXP2_SCALE)
    factor = jnp.exp2((peak_ref[...] - peak) * EXP2_SCALE)
    inverse = 1.0 / (factor * denom_ref[...] + jnp.sum(weights, axis=0, keepdims=True))
    mixed = mixed_ref[...] * (factor * inverse) + mix_values(kv_refs, weights) * inverse
    mixed = mixed.T.astype(jnp.bfloat16)
    heads = width // D_HEAD
    attn = jnp.concatenate([mixed[h * seg : (h + 1) * seg] for h in range(heads)], axis=1)
    attn_ref[...] = attn
    part = project(attn, weight_ref, lax.axis_index("head"), 3, low_ref.shape[1])
    half = low_ref.shape[0]
    low_ref[...] = part[:half]
    high_ref[...] = part[half:]


def attend(kpos, qpos, q_all, kv_chunks, state, weight, n_head):
    n_chunk, (depth, columns) = len(kv_chunks), q_all.shape
    width, out_width = weight.shape
    seg = columns * depth // width
    n_keys = kv_chunks[0].shape[0] * n_chunk
    cols = out_width // n_head
    vmem = pl.BlockSpec(memory_space=pltpu.VMEM)
    half = jax.ShapeDtypeStruct((seg // 2, cols), jnp.bfloat16)
    return pl.pallas_call(
        functools.partial(attend_kernel, n_chunk),
        out_shape=(jax.ShapeDtypeStruct((seg, width), jnp.bfloat16), half, half),
        in_specs=[vmem] * (7 + n_chunk),
        out_specs=(vmem, vmem, vmem),
        compiler_params=pltpu.CompilerParams(vmem_limit_bytes=28 * 1024 * 1024),
        cost_estimate=pl.CostEstimate(
            flops=4 * columns * depth * n_keys + 2 * seg * width * cols,
            bytes_accessed=4 * 1024 * 1024,
            transcendentals=columns * n_keys,
        ),
    )(kpos, qpos, q_all, *kv_chunks, *state, weight)


def project_kernel(flips, attn_ref, weight_ref, *out_refs):
    me = lax.axis_index("head")
    half, cols = out_refs[0].shape
    for i, flip in enumerate(flips):
        part = project(attn_ref[...], weight_ref, me, flip, cols)
        out_refs[2 * i][...] = part[:half]
        out_refs[2 * i + 1][...] = part[half:]


def project_rest(attn, weight, flips, n_head):
    seg, width = attn.shape
    n, cols = len(flips), weight.shape[1] // n_head
    vmem = pl.BlockSpec(memory_space=pltpu.VMEM)
    half = jax.ShapeDtypeStruct((seg // 2, cols), jnp.bfloat16)
    return pl.pallas_call(
        functools.partial(project_kernel, flips),
        out_shape=(half,) * (2 * n),
        in_specs=[vmem, vmem],
        out_specs=(vmem,) * (2 * n),
        compiler_params=pltpu.CompilerParams(vmem_limit_bytes=20 * 1024 * 1024),
        cost_estimate=pl.CostEstimate(
            flops=2 * seg * width * cols * n,
            bytes_accessed=2 * width * cols * n,
            transcendentals=0,
        ),
    )(attn, weight)


def add_kernel(a_ref, b_ref, out_ref):
    out_ref[...] = (a_ref[...].astype(jnp.float32) + b_ref[...].astype(jnp.float32)).astype(jnp.bfloat16)


def add_pair(a, b):
    vmem = pl.BlockSpec(memory_space=pltpu.VMEM)
    return pl.pallas_call(
        add_kernel,
        out_shape=jax.ShapeDtypeStruct(a.shape, jnp.bfloat16),
        in_specs=[vmem, vmem],
        out_specs=vmem,
        compiler_params=pltpu.CompilerParams(vmem_limit_bytes=6 * 1024 * 1024),
        cost_estimate=pl.CostEstimate(flops=a.size, bytes_accessed=6 * a.size, transcendentals=0),
    )(a, b)


def final_kernel(*refs):
    out_ref = refs[-1]
    half = out_ref.shape[0] // 2
    for i in range(2):
        total = sum(ref[...].astype(jnp.float32) for ref in refs[3 * i : 3 * i + 3])
        out_ref[i * half : (i + 1) * half, :] = total.astype(jnp.bfloat16)


def final_sum(low, high):
    vmem = pl.BlockSpec(memory_space=pltpu.VMEM)
    rows, cols = low[0].shape
    return pl.pallas_call(
        final_kernel,
        out_shape=jax.ShapeDtypeStruct((2 * rows, cols), jnp.bfloat16),
        in_specs=[vmem] * 6,
        out_specs=vmem,
        compiler_params=pltpu.CompilerParams(vmem_limit_bytes=6 * 1024 * 1024),
        cost_estimate=pl.CostEstimate(flops=4 * rows * cols, bytes_accessed=16 * rows * cols, transcendentals=0),
    )(*low, *high)


def fast_path(queries, key_rows, value_rows, stretch_order, out_weight, n_head, n_ctx):
    me = lax.axis_index("head")

    def cut(x, k):
        width = x.shape[2] // n_head
        return lax.dynamic_slice_in_dim(x[0], (me ^ k) * width, width, 1)

    kv_cut = [
        jnp.concatenate([cut(key_rows, k), cut(value_rows, k)], axis=1) for k in range(n_head)
    ]
    q_cut = [cut(queries, k) for k in range(n_head)]
    kv_in = [kv_cut[0]] + [swap(kv_cut[k], "head", k, n_head) for k in range(1, n_head)]
    own = jnp.concatenate(kv_in, axis=0)
    q_in = [q_cut[0]] + [swap(q_cut[k], "head", k, n_head) for k in range(1, n_head)]
    flips = [2 * dz for dz in range(n_ctx // 2)]
    chunk_flips = tuple(flips + [f ^ 1 for f in flips])
    weight, qpos, kpos, q_all = prepare(
        stretch_order, out_weight, own, q_in, chunk_flips, own.shape[0] * n_ctx
    )
    far_keys = [swap(own, "ctx", f, n_ctx) for f in flips[1:]]
    far_keys, kpos = lax.optimization_barrier((far_keys, kpos))
    same_core = [own] + far_keys
    other_core = [swap(x, "ctx", 1, n_ctx) for x in same_core]
    state = early_attend(kpos, qpos, q_all, same_core)
    attn, far_low, far_high = attend(kpos, qpos, q_all, other_core, state, weight, n_head)
    x_far = swap(far_low, "head", 1, n_head)
    y_far = swap(far_high, "head", 2, n_head)
    x_low, x_high, y_low, y_high = project_rest(attn, weight, (1, 2), n_head)
    x_near = swap(x_low, "head", 1, n_head)
    y_near = swap(y_high, "head", 2, n_head)
    own_low, own_high = project_rest(attn, weight, (0,), n_head)
    y_sum = swap(add_pair(y_low, x_far), "head", 2, n_head)
    x_sum = swap(add_pair(x_high, y_far), "head", 1, n_head)
    return final_sum((own_low, x_near, y_sum), (own_high, y_near, x_sum))


def attend_block(state, query_heads, query_pos, key_block, value_block, key_pos):
    run_max, run_sum, run_acc = state
    scores = jnp.einsum(
        "tkgd,pkd->kgtp", query_heads, key_block, preferred_element_type=jnp.float32
    ) * D_HEAD ** (-0.5)
    visible = key_pos[None, :] <= query_pos[:, None]
    scores = jnp.where(visible, scores, NEG_FILL)
    new_max = jnp.maximum(run_max, jnp.max(scores, axis=3))
    weights = jnp.where(visible, jnp.exp(scores - new_max[..., None]), 0.0)
    factor = jnp.exp(run_max - new_max)
    new_sum = run_sum * factor + jnp.sum(weights, axis=3)
    product = jnp.einsum(
        "kgtp,pkd->kgtd",
        weights.astype(jnp.bfloat16),
        value_block,
        preferred_element_type=jnp.float32,
    )
    return (new_max, new_sum, run_acc * factor[..., None] + product)


def fold_piece(
    state, query_heads, query_pos, key_piece, value_piece, flat_rows, order, span, kv_heads
):
    count = key_piece.shape[0]
    width = 512 if count % 512 == 0 else count
    blocks_n = count // width
    key_blocks = key_piece.reshape(blocks_n, width, kv_heads, D_HEAD)
    value_blocks = value_piece.reshape(blocks_n, width, kv_heads, D_HEAD)
    flat_blocks = flat_rows.reshape(blocks_n, width)

    def step_block(current, slab):
        key_block, value_block, block_rows = slab
        key_pos = lookup_positions(order, block_rows, span)
        return (
            attend_block(current, query_heads, query_pos, key_block, value_block, key_pos),
            None,
        )

    state, unused = lax.scan(step_block, state, (key_blocks, value_blocks, flat_blocks))
    return state


def long_path(queries, key_rows, value_rows, stretch_order, out_weight, n_head):
    ctx_index = lax.axis_index("ctx")
    span = queries.shape[1]
    seg_rows = span * n_head
    kv_local = key_rows.shape[2] // D_HEAD // n_head
    q_local = queries.shape[2] // D_HEAD // n_head
    groups = q_local // kv_local
    query_flat = ctx_index * seg_rows + jnp.arange(seg_rows, dtype=jnp.int32)
    query_pos = lookup_positions(stretch_order, query_flat, span)
    initial = (
        jnp.full((kv_local, groups, seg_rows), NEG_FILL, jnp.float32),
        jnp.zeros((kv_local, groups, seg_rows), jnp.float32),
        jnp.zeros((kv_local, groups, seg_rows, D_HEAD), jnp.float32),
    )
    query_ex, key_ex, value_ex = (
        lax.all_to_all(queries, "head", split_axis=2, concat_axis=1, tiled=True),
        lax.all_to_all(key_rows, "head", split_axis=2, concat_axis=1, tiled=True),
        lax.all_to_all(value_rows, "head", split_axis=2, concat_axis=1, tiled=True),
    )
    query_heads = query_ex[0].reshape(seg_rows, kv_local, groups, D_HEAD)
    keys = lax.all_gather(key_ex[0], "ctx", axis=0, tiled=True)
    values = lax.all_gather(value_ex[0], "ctx", axis=0, tiled=True)
    flat_rows = jnp.arange(keys.shape[0], dtype=jnp.int32)
    final = fold_piece(
        initial, query_heads, query_pos, keys, values, flat_rows, stretch_order, span, kv_local
    )
    run_max, run_sum, run_acc = final
    mixed = run_acc / run_sum[..., None]
    attn = (
        jnp.transpose(mixed, (2, 0, 1, 3)).reshape(seg_rows, q_local * D_HEAD).astype(jnp.bfloat16)
    )
    partial_out = jnp.dot(attn, out_weight, preferred_element_type=jnp.float32).astype(jnp.bfloat16)
    return (
        lax.psum_scatter(partial_out, "head", scatter_dimension=1, tiled=True)
        .astype(jnp.float32)
        .astype(jnp.bfloat16)
    )


def solution(mesh):
    n_head, n_ctx = mesh.shape["head"], mesh.shape["ctx"]

    def on_device(*args):
        if n_ctx <= 8:
            return fast_path(*args, n_head, n_ctx)
        return long_path(*args, n_head)

    return jax.shard_map(
        on_device,
        mesh=mesh,
        in_specs=(
            P("ctx", "head", None),
            P("ctx", "head", None),
            P("ctx", "head", None),
            P(),
            P("head", None),
        ),
        out_specs=P("ctx", "head"),
        check_vma=False,
    )
```

```python
import functools
import math

import jax
import jax.numpy as jnp
from jax import lax
from jax.experimental import pallas as pl
from jax.experimental.pallas import tpu as pltpu
from jax.sharding import PartitionSpec as P

D_HEAD = 128
NEG_FILL = -1e30
ROOMY = 42
STRIPE = 256
FETCHES = 8
EXP2_SCALE = D_HEAD ** (-0.5) * math.log2(math.e)


def swap(x, axis, flip, size):
    return lax.ppermute(x, axis, [(i, i ^ flip) for i in range(size)])


def swap_by_core(x, flips, n_head, n_ctx):
    pairs = [
        (j * n_ctx + c, (j ^ flips[c % 2]) * n_ctx + c) for j in range(n_head) for c in range(n_ctx)
    ]
    return lax.ppermute(x, ("head", "ctx"), pairs)


def first_flip():
    return 1 + lax.rem(lax.axis_index("ctx"), 2)


def lookup_positions(order, flat_rows, span):
    table = jnp.arange(order.shape[0], dtype=jnp.int32)
    hits = (flat_rows // span)[:, None] == table[None, :]
    return jnp.sum(jnp.where(hits, order[None, :], 0), axis=1) * span + flat_rows % span


def prepare_kernel(span, n_head, chunk_flips, order_ref, weight_ref, after_ref, *refs):
    q_refs, (weight_out, qpos_ref, kpos_ref, q_out, q_s, sems) = refs[:n_head], refs[n_head:]
    me, ctx = lax.axis_index("head"), lax.axis_index("ctx")
    step = weight_ref.shape[0] // FETCHES
    fetches = [
        pltpu.make_async_copy(
            weight_ref.at[i * step : (i + 1) * step], weight_out.at[i * step : (i + 1) * step], sems.at[i]
        )
        for i in range(FETCHES)
    ]

    @pl.when(me >= 0)
    def start():
        for fetch in fetches:
            fetch.start()

    row = lax.broadcasted_iota(jnp.int32, (span, D_HEAD), 0)
    for i, flip in enumerate(chunk_flips):
        for k in range(n_head):
            first = (i * n_head + k) * span
            block = order_ref[(ctx ^ flip) * n_head + (me ^ k)]
            kpos_ref[first : first + span, :] = row + block * span
    heads = q_refs[0].shape[1] // D_HEAD
    lane = lax.broadcasted_iota(jnp.int32, qpos_ref.shape, 1)
    qpos = lane
    for i in range(heads * n_head):
        block = order_ref[ctx * n_head + i % n_head]
        qpos = jnp.where(lane >= i * span, lane + (block - i) * span, qpos)
    qpos_ref[...] = qpos
    for k in range(n_head):
        at = pl.multiple_of((me ^ k) * span, span)
        q_s[pl.ds(at, span), :] = q_refs[k][...].astype(jnp.float32)
    stacked = jnp.concatenate([q_s[:, h * D_HEAD : (h + 1) * D_HEAD] for h in range(heads)], axis=0)
    q_out[...] = stacked.T.astype(jnp.bfloat16)
    for fetch in fetches:
        fetch.wait()


def prepare(order, weight, after, q_pieces, chunk_flips, n_keys):
    n_head = len(q_pieces)
    span, width = q_pieces[0].shape
    columns = span * n_head * width // D_HEAD
    vmem = pl.BlockSpec(memory_space=pltpu.VMEM)
    return pl.pallas_call(
        functools.partial(prepare_kernel, span, n_head, chunk_flips),
        out_shape=(
            jax.ShapeDtypeStruct(weight.shape, weight.dtype),
            jax.ShapeDtypeStruct((1, columns), jnp.int32),
            jax.ShapeDtypeStruct((n_keys, D_HEAD), jnp.int32),
            jax.ShapeDtypeStruct((D_HEAD, columns), jnp.bfloat16),
        ),
        in_specs=[
            pl.BlockSpec(memory_space=pltpu.SMEM),
            pl.BlockSpec(memory_space=pltpu.HBM),
            pl.BlockSpec(memory_space=pl.ANY),
        ]
        + [vmem] * n_head,
        out_specs=(vmem,) * 4,
        scratch_shapes=[
            pltpu.VMEM((span * n_head, width), jnp.float32),
            pltpu.SemaphoreType.DMA((FETCHES,)),
        ],
        compiler_params=pltpu.CompilerParams(vmem_limit_bytes=ROOMY * 1024 * 1024),
        cost_estimate=pl.CostEstimate(flops=0, bytes_accessed=4 * 1024 * 1024, transcendentals=0),
    )(order, weight, after, *q_pieces)


def project(attn, weight_ref, flip, cols):
    at = pl.multiple_of((lax.axis_index("head") ^ flip) * cols, cols)
    part = jnp.dot(attn, weight_ref[:, pl.ds(at, cols)], preferred_element_type=jnp.float32)
    return part.astype(jnp.bfloat16)


def fold_keys(kv_refs, kpos, qpos_ref, q_ref, state, emit):
    keys = jnp.concatenate([ref[:, :D_HEAD] for ref in kv_refs], axis=0)
    values = jnp.concatenate([ref[:, D_HEAD:] for ref in kv_refs], axis=0).T
    kpos = jnp.concatenate([kpos] * (STRIPE // D_HEAD), axis=1)

    def score(at):
        scores = jnp.dot(keys, q_ref[:, at], preferred_element_type=jnp.float32)
        return jnp.where(kpos <= qpos_ref[:, at], scores, NEG_FILL)

    def weigh(at, scores):
        peak = jnp.max(scores, axis=0, keepdims=True)
        if state is not None:
            peak = jnp.maximum(state[0][:, at], peak)
        weights = jnp.exp2((scores - peak) * EXP2_SCALE)
        return peak, jnp.sum(weights, axis=0, keepdims=True), weights.astype(jnp.bfloat16)

    def finish(at, peak, denom, weights):
        mixed = jnp.dot(values, weights, preferred_element_type=jnp.float32)
        if state is not None:
            factor = jnp.exp2((state[0][:, at] - peak) * EXP2_SCALE)
            denom = factor * state[1][:, at] + denom
            mixed = factor * state[2][:, at] + mixed
        emit(at, peak, denom, mixed)

    stripes = [slice(i, i + STRIPE) for i in range(0, q_ref.shape[1], STRIPE)]
    scores, held = score(stripes[0]), None
    for i, at in enumerate(stripes):
        ahead = score(stripes[i + 1]) if i + 1 < len(stripes) else None
        weighed = weigh(at, scores)
        if held is not None:
            finish(stripes[i - 1], *held)
        scores, held = ahead, weighed
    finish(stripes[-1], *held)


def early_kernel(n_chunk, kpos_ref, qpos_ref, q_ref, *refs):
    kv_refs, out = refs[:n_chunk], refs[n_chunk:]
    n_keys = kv_refs[0].shape[0] * n_chunk

    def emit(at, peak, denom, mixed):
        for ref, value in zip(out, (peak, denom, mixed), strict=True):
            ref[:, at] = value

    fold_keys(kv_refs, kpos_ref[:n_keys, :], qpos_ref, q_ref, None, emit)


def early_attend(kpos, qpos, q_all, kv_chunks):
    n_chunk, (depth, columns) = len(kv_chunks), q_all.shape
    n_keys = kv_chunks[0].shape[0] * n_chunk
    vmem = pl.BlockSpec(memory_space=pltpu.VMEM)
    line = jax.ShapeDtypeStruct((1, columns), jnp.float32)
    return pl.pallas_call(
        functools.partial(early_kernel, n_chunk),
        out_shape=(line, line, jax.ShapeDtypeStruct((depth, columns), jnp.float32)),
        in_specs=[vmem] * (3 + n_chunk),
        out_specs=(vmem,) * 3,
        compiler_params=pltpu.CompilerParams(vmem_limit_bytes=20 * 1024 * 1024),
        cost_estimate=pl.CostEstimate(
            flops=4 * columns * depth * n_keys,
            bytes_accessed=4 * 1024 * 1024,
            transcendentals=columns * n_keys,
        ),
    )(kpos, qpos, q_all, *kv_chunks)


def attend_kernel(n_chunk, kpos_ref, qpos_ref, q_ref, *refs):
    kv_refs, state = refs[:n_chunk], refs[n_chunk : n_chunk + 3]
    weight_ref, attn_ref, far_ref = refs[n_chunk + 3 :]
    seg, width = attn_ref.shape
    n_keys = kv_refs[0].shape[0] * n_chunk
    rows = []

    def emit(at, peak, denom, mixed):
        rows.append((mixed * (1.0 / denom)).T.astype(jnp.bfloat16))

    fold_keys(kv_refs, kpos_ref[n_keys:, :], qpos_ref, q_ref, state, emit)
    rows = jnp.concatenate(rows, axis=0)
    heads = width // D_HEAD
    attn = jnp.concatenate([rows[h * seg : (h + 1) * seg] for h in range(heads)], axis=1)
    attn_ref[...] = attn
    far_ref[...] = project(attn, weight_ref, 3, far_ref.shape[1])


def attend(kpos, qpos, q_all, kv_chunks, state, weight, n_head):
    n_chunk, (depth, columns) = len(kv_chunks), q_all.shape
    width, out_width = weight.shape
    seg = columns * depth // width
    n_keys = kv_chunks[0].shape[0] * n_chunk
    cols = out_width // n_head
    vmem = pl.BlockSpec(memory_space=pltpu.VMEM)
    return pl.pallas_call(
        functools.partial(attend_kernel, n_chunk),
        out_shape=(
            jax.ShapeDtypeStruct((seg, width), jnp.bfloat16),
            jax.ShapeDtypeStruct((seg, cols), jnp.bfloat16),
        ),
        in_specs=[vmem] * (7 + n_chunk),
        out_specs=(vmem, vmem),
        compiler_params=pltpu.CompilerParams(vmem_limit_bytes=28 * 1024 * 1024),
        cost_estimate=pl.CostEstimate(
            flops=4 * columns * depth * n_keys + 2 * seg * width * cols,
            bytes_accessed=4 * 1024 * 1024,
            transcendentals=columns * n_keys,
        ),
    )(kpos, qpos, q_all, *kv_chunks, *state, weight)


def near_kernel(attn_ref, weight_ref, first_ref, second_ref):
    flip = first_flip()
    first_ref[...] = project(attn_ref[...], weight_ref, flip, first_ref.shape[1])
    second_ref[...] = project(attn_ref[...], weight_ref, 3 - flip, first_ref.shape[1])


def own_kernel(attn_ref, weight_ref, out_ref):
    out_ref[...] = project(attn_ref[...], weight_ref, 0, out_ref.shape[1])


def project_rest(kernel, n, attn, weight, n_head):
    seg, width = attn.shape
    cols = weight.shape[1] // n_head
    vmem = pl.BlockSpec(memory_space=pltpu.VMEM)
    return pl.pallas_call(
        kernel,
        out_shape=(jax.ShapeDtypeStruct((seg, cols), jnp.bfloat16),) * n,
        in_specs=[vmem, vmem],
        out_specs=(vmem,) * n,
        compiler_params=pltpu.CompilerParams(vmem_limit_bytes=20 * 1024 * 1024),
        cost_estimate=pl.CostEstimate(
            flops=2 * seg * width * cols * n,
            bytes_accessed=2 * width * cols * n,
            transcendentals=0,
        ),
    )(attn, weight)


def sum_kernel(*refs):
    total = sum(ref[...].astype(jnp.float32) for ref in refs[:-1])
    refs[-1][...] = total.astype(jnp.bfloat16)


def sum_blocks(*blocks):
    vmem = pl.BlockSpec(memory_space=pltpu.VMEM)
    size = blocks[0].size * len(blocks)
    return pl.pallas_call(
        sum_kernel,
        out_shape=jax.ShapeDtypeStruct(blocks[0].shape, jnp.bfloat16),
        in_specs=[vmem] * len(blocks),
        out_specs=vmem,
        compiler_params=pltpu.CompilerParams(vmem_limit_bytes=6 * 1024 * 1024),
        cost_estimate=pl.CostEstimate(flops=size, bytes_accessed=2 * size, transcendentals=0),
    )(*blocks)


def fast_path(queries, key_rows, value_rows, stretch_order, out_weight, n_head, n_ctx):
    me = lax.axis_index("head")

    def cut(x, k):
        width = x.shape[2] // n_head
        return lax.dynamic_slice_in_dim(x[0], (me ^ k) * width, width, 1)

    kv_cut = [
        jnp.concatenate([cut(key_rows, k), cut(value_rows, k)], axis=1) for k in range(n_head)
    ]
    q_cut = [cut(queries, k) for k in range(n_head)]
    kv_in = [kv_cut[0]] + [swap(kv_cut[k], "head", k, n_head) for k in range(1, n_head)]
    own = jnp.concatenate(kv_in, axis=0)
    q_in = [q_cut[0]] + [swap(q_cut[k], "head", k, n_head) for k in range(1, n_head)]
    flips = [2 * dz for dz in range(n_ctx // 2)]
    chunk_flips = tuple(flips + [f ^ 1 for f in flips])
    weight, qpos, kpos, q_all = prepare(
        stretch_order, out_weight, own, q_in, chunk_flips, own.shape[0] * n_ctx
    )
    far_keys = [swap(own, "ctx", f, n_ctx) for f in flips[1:]]
    far_keys, kpos = lax.optimization_barrier((far_keys, kpos))
    same_core = [own] + far_keys
    other_core = [swap(x, "ctx", 1, n_ctx) for x in same_core]
    state = early_attend(kpos, qpos, q_all, same_core)
    attn, far = attend(kpos, qpos, q_all, other_core, state, weight, n_head)
    passed = swap_by_core(far, (1, 2), n_head, n_ctx)
    first, second = project_rest(near_kernel, 2, attn, weight, n_head)
    received = swap_by_core(first, (1, 2), n_head, n_ctx)
    (kept,) = project_rest(own_kernel, 1, attn, weight, n_head)
    joined = swap_by_core(sum_blocks(second, passed), (2, 1), n_head, n_ctx)
    return sum_blocks(kept, received, joined)


def attend_block(state, query_heads, query_pos, key_block, value_block, key_pos):
    run_max, run_sum, run_acc = state
    scores = jnp.einsum(
        "tkgd,pkd->kgtp", query_heads, key_block, preferred_element_type=jnp.float32
    ) * D_HEAD ** (-0.5)
    visible = key_pos[None, :] <= query_pos[:, None]
    scores = jnp.where(visible, scores, NEG_FILL)
    new_max = jnp.maximum(run_max, jnp.max(scores, axis=3))
    weights = jnp.where(visible, jnp.exp(scores - new_max[..., None]), 0.0)
    factor = jnp.exp(run_max - new_max)
    new_sum = run_sum * factor + jnp.sum(weights, axis=3)
    product = jnp.einsum(
        "kgtp,pkd->kgtd",
        weights.astype(jnp.bfloat16),
        value_block,
        preferred_element_type=jnp.float32,
    )
    return (new_max, new_sum, run_acc * factor[..., None] + product)


def fold_piece(
    state, query_heads, query_pos, key_piece, value_piece, flat_rows, order, span, kv_heads
):
    count = key_piece.shape[0]
    width = 512 if count % 512 == 0 else count
    blocks_n = count // width
    key_blocks = key_piece.reshape(blocks_n, width, kv_heads, D_HEAD)
    value_blocks = value_piece.reshape(blocks_n, width, kv_heads, D_HEAD)
    flat_blocks = flat_rows.reshape(blocks_n, width)

    def step_block(current, slab):
        key_block, value_block, block_rows = slab
        key_pos = lookup_positions(order, block_rows, span)
        return (
            attend_block(current, query_heads, query_pos, key_block, value_block, key_pos),
            None,
        )

    state, unused = lax.scan(step_block, state, (key_blocks, value_blocks, flat_blocks))
    return state


def long_path(queries, key_rows, value_rows, stretch_order, out_weight, n_head):
    ctx_index = lax.axis_index("ctx")
    span = queries.shape[1]
    seg_rows = span * n_head
    kv_local = key_rows.shape[2] // D_HEAD // n_head
    q_local = queries.shape[2] // D_HEAD // n_head
    groups = q_local // kv_local
    query_flat = ctx_index * seg_rows + jnp.arange(seg_rows, dtype=jnp.int32)
    query_pos = lookup_positions(stretch_order, query_flat, span)
    initial = (
        jnp.full((kv_local, groups, seg_rows), NEG_FILL, jnp.float32),
        jnp.zeros((kv_local, groups, seg_rows), jnp.float32),
        jnp.zeros((kv_local, groups, seg_rows, D_HEAD), jnp.float32),
    )
    query_ex, key_ex, value_ex = (
        lax.all_to_all(queries, "head", split_axis=2, concat_axis=1, tiled=True),
        lax.all_to_all(key_rows, "head", split_axis=2, concat_axis=1, tiled=True),
        lax.all_to_all(value_rows, "head", split_axis=2, concat_axis=1, tiled=True),
    )
    query_heads = query_ex[0].reshape(seg_rows, kv_local, groups, D_HEAD)
    keys = lax.all_gather(key_ex[0], "ctx", axis=0, tiled=True)
    values = lax.all_gather(value_ex[0], "ctx", axis=0, tiled=True)
    flat_rows = jnp.arange(keys.shape[0], dtype=jnp.int32)
    final = fold_piece(
        initial, query_heads, query_pos, keys, values, flat_rows, stretch_order, span, kv_local
    )
    run_max, run_sum, run_acc = final
    mixed = run_acc / run_sum[..., None]
    attn = (
        jnp.transpose(mixed, (2, 0, 1, 3)).reshape(seg_rows, q_local * D_HEAD).astype(jnp.bfloat16)
    )
    partial_out = jnp.dot(attn, out_weight, preferred_element_type=jnp.float32).astype(jnp.bfloat16)
    return (
        lax.psum_scatter(partial_out, "head", scatter_dimension=1, tiled=True)
        .astype(jnp.float32)
        .astype(jnp.bfloat16)
    )


def solution(mesh):
    n_head, n_ctx = mesh.shape["head"], mesh.shape["ctx"]

    def on_device(*args):
        if n_ctx <= 8:
            return fast_path(*args, n_head, n_ctx)
        return long_path(*args, n_head)

    return jax.shard_map(
        on_device,
        mesh=mesh,
        in_specs=(
            P("ctx", "head", None),
            P("ctx", "head", None),
            P("ctx", "head", None),
            P(),
            P("head", None),
        ),
        out_specs=P("ctx", "head"),
        check_vma=False,
    )
```

```python
import functools
import math

import jax
import jax.numpy as jnp
from jax import lax
from jax.experimental import pallas as pl
from jax.experimental.pallas import tpu as pltpu
from jax.sharding import PartitionSpec as P

D_HEAD = 128
NEG_FILL = -1e30
ROOMY = 42
STRIPE = 256
FETCHES = 8
PARTS = 2
EXP2_SCALE = D_HEAD ** (-0.5) * math.log2(math.e)


def swap(x, axis, flip, size):
    return lax.ppermute(x, axis, [(i, i ^ flip) for i in range(size)])


def swap_by_core(x, flips, n_head, n_ctx):
    pairs = [
        (j * n_ctx + c, (j ^ flips[c % 2]) * n_ctx + c) for j in range(n_head) for c in range(n_ctx)
    ]
    return lax.ppermute(x, ("head", "ctx"), pairs)


def first_flip():
    return 1 + lax.rem(lax.axis_index("ctx"), 2)


def lookup_positions(order, flat_rows, span):
    table = jnp.arange(order.shape[0], dtype=jnp.int32)
    hits = (flat_rows // span)[:, None] == table[None, :]
    return jnp.sum(jnp.where(hits, order[None, :], 0), axis=1) * span + flat_rows % span


def prepare_kernel(span, n_head, chunk_flips, order_ref, weight_ref, after_ref, *refs):
    q_refs, (weight_out, qpos_ref, kpos_ref, q_out, q_s, sems) = refs[:n_head], refs[n_head:]
    me, ctx = lax.axis_index("head"), lax.axis_index("ctx")
    step = weight_ref.shape[0] // FETCHES
    fetches = [
        pltpu.make_async_copy(
            weight_ref.at[i * step : (i + 1) * step], weight_out.at[i * step : (i + 1) * step], sems.at[i]
        )
        for i in range(FETCHES)
    ]

    @pl.when(me >= 0)
    def start():
        for fetch in fetches:
            fetch.start()

    row = lax.broadcasted_iota(jnp.int32, (span, D_HEAD), 0)
    for i, flip in enumerate(chunk_flips):
        for k in range(n_head):
            first = (i * n_head + k) * span
            block = order_ref[(ctx ^ flip) * n_head + (me ^ k)]
            kpos_ref[first : first + span, :] = row + block * span
    heads = q_refs[0].shape[1] // D_HEAD
    lane = lax.broadcasted_iota(jnp.int32, qpos_ref.shape, 1)
    qpos = lane
    for i in range(heads * n_head):
        block = order_ref[ctx * n_head + i % n_head]
        qpos = jnp.where(lane >= i * span, lane + (block - i) * span, qpos)
    qpos_ref[...] = qpos
    for k in range(n_head):
        at = pl.multiple_of((me ^ k) * span, span)
        q_s[pl.ds(at, span), :] = q_refs[k][...].astype(jnp.float32)
    stacked = jnp.concatenate([q_s[:, h * D_HEAD : (h + 1) * D_HEAD] for h in range(heads)], axis=0)
    q_out[...] = stacked.T.astype(jnp.bfloat16)
    for fetch in fetches:
        fetch.wait()


def prepare(order, weight, after, q_pieces, chunk_flips, n_keys):
    n_head = len(q_pieces)
    span, width = q_pieces[0].shape
    columns = span * n_head * width // D_HEAD
    vmem = pl.BlockSpec(memory_space=pltpu.VMEM)
    return pl.pallas_call(
        functools.partial(prepare_kernel, span, n_head, chunk_flips),
        out_shape=(
            jax.ShapeDtypeStruct(weight.shape, weight.dtype),
            jax.ShapeDtypeStruct((1, columns), jnp.int32),
            jax.ShapeDtypeStruct((n_keys, D_HEAD), jnp.int32),
            jax.ShapeDtypeStruct((D_HEAD, columns), jnp.bfloat16),
        ),
        in_specs=[
            pl.BlockSpec(memory_space=pltpu.SMEM),
            pl.BlockSpec(memory_space=pltpu.HBM),
            pl.BlockSpec(memory_space=pl.ANY),
        ]
        + [vmem] * n_head,
        out_specs=(vmem,) * 4,
        scratch_shapes=[
            pltpu.VMEM((span * n_head, width), jnp.float32),
            pltpu.SemaphoreType.DMA((FETCHES,)),
        ],
        compiler_params=pltpu.CompilerParams(vmem_limit_bytes=ROOMY * 1024 * 1024),
        cost_estimate=pl.CostEstimate(flops=0, bytes_accessed=4 * 1024 * 1024, transcendentals=0),
    )(order, weight, after, *q_pieces)


def project(attn, weight_ref, flip, cols):
    at = pl.multiple_of((lax.axis_index("head") ^ flip) * cols, cols)
    part = jnp.dot(attn, weight_ref[:, pl.ds(at, cols)], preferred_element_type=jnp.float32)
    return part.astype(jnp.bfloat16)


def fold_keys(kv_refs, kpos, qpos_ref, q_ref, state, emit):
    keys = jnp.concatenate([ref[:, :D_HEAD] for ref in kv_refs], axis=0)
    values = jnp.concatenate([ref[:, D_HEAD:] for ref in kv_refs], axis=0).T
    kpos = jnp.concatenate([kpos] * (STRIPE // D_HEAD), axis=1)

    def score(at):
        scores = jnp.dot(keys, q_ref[:, at], preferred_element_type=jnp.float32)
        return jnp.where(kpos <= qpos_ref[:, at], scores, NEG_FILL)

    def weigh(at, scores):
        peak = jnp.max(scores, axis=0, keepdims=True)
        if state is not None:
            peak = jnp.maximum(state[0][:, at], peak)
        weights = jnp.exp2((scores - peak) * EXP2_SCALE)
        return peak, jnp.sum(weights, axis=0, keepdims=True), weights.astype(jnp.bfloat16)

    def finish(at, peak, denom, weights):
        mixed = jnp.dot(values, weights, preferred_element_type=jnp.float32)
        if state is not None:
            factor = jnp.exp2((state[0][:, at] - peak) * EXP2_SCALE)
            denom = factor * state[1][:, at] + denom
            mixed = factor * state[2][:, at] + mixed
        emit(at, peak, denom, mixed)

    stripes = [slice(i, i + STRIPE) for i in range(0, q_ref.shape[1], STRIPE)]
    scores, held = score(stripes[0]), None
    for i, at in enumerate(stripes):
        ahead = score(stripes[i + 1]) if i + 1 < len(stripes) else None
        weighed = weigh(at, scores)
        if held is not None:
            finish(stripes[i - 1], *held)
        scores, held = ahead, weighed
    finish(stripes[-1], *held)


def early_kernel(n_chunk, kpos_ref, qpos_ref, q_ref, *refs):
    kv_refs, out = refs[:n_chunk], refs[n_chunk:]
    n_keys = sum(ref.shape[0] for ref in kv_refs)

    def emit(at, peak, denom, mixed):
        for ref, value in zip(out, (peak, denom, mixed), strict=True):
            ref[:, at] = value

    fold_keys(kv_refs, kpos_ref[:n_keys, :], qpos_ref, q_ref, None, emit)


def early_attend(kpos, qpos, q_all, kv_chunks):
    n_chunk, (depth, columns) = len(kv_chunks), q_all.shape
    n_keys = sum(chunk.shape[0] for chunk in kv_chunks)
    vmem = pl.BlockSpec(memory_space=pltpu.VMEM)
    line = jax.ShapeDtypeStruct((1, columns), jnp.float32)
    return pl.pallas_call(
        functools.partial(early_kernel, n_chunk),
        out_shape=(line, line, jax.ShapeDtypeStruct((depth, columns), jnp.float32)),
        in_specs=[vmem] * (3 + n_chunk),
        out_specs=(vmem,) * 3,
        compiler_params=pltpu.CompilerParams(vmem_limit_bytes=20 * 1024 * 1024),
        cost_estimate=pl.CostEstimate(
            flops=4 * columns * depth * n_keys,
            bytes_accessed=4 * 1024 * 1024,
            transcendentals=columns * n_keys,
        ),
    )(kpos, qpos, q_all, *kv_chunks)


def attend_kernel(n_chunk, kpos_ref, qpos_ref, q_ref, *refs):
    kv_refs, state = refs[:n_chunk], refs[n_chunk : n_chunk + 3]
    weight_ref, attn_ref, *far_refs = refs[n_chunk + 3 :]
    seg, width = attn_ref.shape
    n_keys = sum(ref.shape[0] for ref in kv_refs)
    rows = []

    def emit(at, peak, denom, mixed):
        rows.append((mixed * (1.0 / denom)).T.astype(jnp.bfloat16))

    fold_keys(kv_refs, kpos_ref[n_keys:, :], qpos_ref, q_ref, state, emit)
    rows = jnp.concatenate(rows, axis=0)
    heads = width // D_HEAD
    attn = jnp.concatenate([rows[h * seg : (h + 1) * seg] for h in range(heads)], axis=1)
    attn_ref[...] = attn
    split_rows(project(attn, weight_ref, 3, far_refs[0].shape[1]), far_refs)


def attend(kpos, qpos, q_all, kv_chunks, state, weight, n_head):
    n_chunk, (depth, columns) = len(kv_chunks), q_all.shape
    width, out_width = weight.shape
    seg = columns * depth // width
    n_keys = sum(chunk.shape[0] for chunk in kv_chunks)
    cols = out_width // n_head
    vmem = pl.BlockSpec(memory_space=pltpu.VMEM)
    return pl.pallas_call(
        functools.partial(attend_kernel, n_chunk),
        out_shape=(
            jax.ShapeDtypeStruct((seg, width), jnp.bfloat16),
            *(jax.ShapeDtypeStruct((seg // PARTS, cols), jnp.bfloat16),) * PARTS,
        ),
        in_specs=[vmem] * (7 + n_chunk),
        out_specs=(vmem,) * (1 + PARTS),
        compiler_params=pltpu.CompilerParams(vmem_limit_bytes=28 * 1024 * 1024),
        cost_estimate=pl.CostEstimate(
            flops=4 * columns * depth * n_keys + 2 * seg * width * cols,
            bytes_accessed=4 * 1024 * 1024,
            transcendentals=columns * n_keys,
        ),
    )(kpos, qpos, q_all, *kv_chunks, *state, weight)


def split_rows(block, refs):
    rows = refs[0].shape[0]
    for i, ref in enumerate(refs):
        ref[...] = block[i * rows : (i + 1) * rows]


def near_kernel(attn_ref, weight_ref, first_ref, *second_refs):
    flip, cols = first_flip(), first_ref.shape[1]
    first_ref[...] = project(attn_ref[...], weight_ref, flip, cols)
    split_rows(project(attn_ref[...], weight_ref, 3 - flip, cols), second_refs)


def own_kernel(attn_ref, weight_ref, out_ref):
    out_ref[...] = project(attn_ref[...], weight_ref, 0, out_ref.shape[1])


def project_rest(kernel, out_rows, attn, weight, n_head):
    seg, width = attn.shape
    cols = weight.shape[1] // n_head
    vmem = pl.BlockSpec(memory_space=pltpu.VMEM)
    return pl.pallas_call(
        kernel,
        out_shape=tuple(jax.ShapeDtypeStruct((rows, cols), jnp.bfloat16) for rows in out_rows),
        in_specs=[vmem, vmem],
        out_specs=(vmem,) * len(out_rows),
        compiler_params=pltpu.CompilerParams(vmem_limit_bytes=20 * 1024 * 1024),
        cost_estimate=pl.CostEstimate(
            flops=2 * sum(out_rows) * width * cols,
            bytes_accessed=2 * width * cols,
            transcendentals=0,
        ),
    )(attn, weight)


def sum_kernel(mine_ref, theirs_ref, out_ref):
    total = mine_ref[...].astype(jnp.float32) + theirs_ref[...].astype(jnp.float32)
    out_ref[...] = total.astype(jnp.bfloat16)


def final_kernel(kept_ref, received_ref, *refs):
    out_ref = refs[-1]
    rows = refs[0].shape[0]
    for i, ref in enumerate(refs[:-1]):
        at = slice(i * rows, (i + 1) * rows)
        total = kept_ref[at].astype(jnp.float32) + received_ref[at].astype(jnp.float32)
        out_ref[at] = (total + ref[...].astype(jnp.float32)).astype(jnp.bfloat16)


def sum_blocks(kernel, *blocks):
    vmem = pl.BlockSpec(memory_space=pltpu.VMEM)
    size = blocks[0].size * len(blocks)
    return pl.pallas_call(
        kernel,
        out_shape=jax.ShapeDtypeStruct(blocks[0].shape, jnp.bfloat16),
        in_specs=[vmem] * len(blocks),
        out_specs=vmem,
        compiler_params=pltpu.CompilerParams(vmem_limit_bytes=6 * 1024 * 1024),
        cost_estimate=pl.CostEstimate(flops=size, bytes_accessed=2 * size, transcendentals=0),
    )(*blocks)


def fast_path(queries, key_rows, value_rows, stretch_order, out_weight, n_head, n_ctx):
    me = lax.axis_index("head")

    def cut(x, k):
        width = x.shape[2] // n_head
        return lax.dynamic_slice_in_dim(x[0], (me ^ k) * width, width, 1)

    kv_cut = [
        jnp.concatenate([cut(key_rows, k), cut(value_rows, k)], axis=1) for k in range(n_head)
    ]
    q_cut = [cut(queries, k) for k in range(n_head)]
    kv_in = [kv_cut[0]] + [swap(kv_cut[k], "head", k, n_head) for k in range(1, n_head)]
    own = jnp.concatenate(kv_in, axis=0)
    q_in = [q_cut[0]] + [swap(q_cut[k], "head", k, n_head) for k in range(1, n_head)]
    flips = [2 * dz for dz in range(n_ctx // 2)]
    seg = own.shape[0]
    chunk_flips = tuple(flips + [f ^ 1 for f in flips])
    weight, qpos, kpos, q_all = prepare(
        stretch_order, out_weight, own, q_in, chunk_flips, own.shape[0] * n_ctx
    )
    far_keys = [swap(own, "ctx", f, n_ctx) for f in flips[1:]]
    far_keys, kpos = lax.optimization_barrier((far_keys, kpos))
    same_core = [own] + far_keys
    other_core = [swap(own, "ctx", 1, n_ctx), swap(jnp.concatenate(far_keys, axis=0), "ctx", 1, n_ctx)]
    state = early_attend(kpos, qpos, q_all, same_core)
    attn, *far = attend(kpos, qpos, q_all, other_core, state, weight, n_head)
    passed = [swap_by_core(x, (1, 2), n_head, n_ctx) for x in far]
    half = seg // PARTS
    first, *second = project_rest(near_kernel, (seg,) + (half,) * PARTS, attn, weight, n_head)
    received = swap_by_core(first, (1, 2), n_head, n_ctx)
    (kept,) = project_rest(own_kernel, (seg,), attn, weight, n_head)
    joined = [
        swap_by_core(sum_blocks(sum_kernel, mine, theirs), (2, 1), n_head, n_ctx)
        for mine, theirs in zip(second, passed, strict=True)
    ]
    return sum_blocks(final_kernel, kept, received, *joined)


def attend_block(state, query_heads, query_pos, key_block, value_block, key_pos):
    run_max, run_sum, run_acc = state
    scores = jnp.einsum(
        "tkgd,pkd->kgtp", query_heads, key_block, preferred_element_type=jnp.float32
    ) * D_HEAD ** (-0.5)
    visible = key_pos[None, :] <= query_pos[:, None]
    scores = jnp.where(visible, scores, NEG_FILL)
    new_max = jnp.maximum(run_max, jnp.max(scores, axis=3))
    weights = jnp.where(visible, jnp.exp(scores - new_max[..., None]), 0.0)
    factor = jnp.exp(run_max - new_max)
    new_sum = run_sum * factor + jnp.sum(weights, axis=3)
    product = jnp.einsum(
        "kgtp,pkd->kgtd",
        weights.astype(jnp.bfloat16),
        value_block,
        preferred_element_type=jnp.float32,
    )
    return (new_max, new_sum, run_acc * factor[..., None] + product)


def fold_piece(
    state, query_heads, query_pos, key_piece, value_piece, flat_rows, order, span, kv_heads
):
    count = key_piece.shape[0]
    width = 512 if count % 512 == 0 else count
    blocks_n = count // width
    key_blocks = key_piece.reshape(blocks_n, width, kv_heads, D_HEAD)
    value_blocks = value_piece.reshape(blocks_n, width, kv_heads, D_HEAD)
    flat_blocks = flat_rows.reshape(blocks_n, width)

    def step_block(current, slab):
        key_block, value_block, block_rows = slab
        key_pos = lookup_positions(order, block_rows, span)
        return (
            attend_block(current, query_heads, query_pos, key_block, value_block, key_pos),
            None,
        )

    state, unused = lax.scan(step_block, state, (key_blocks, value_blocks, flat_blocks))
    return state


def long_path(queries, key_rows, value_rows, stretch_order, out_weight, n_head):
    ctx_index = lax.axis_index("ctx")
    span = queries.shape[1]
    seg_rows = span * n_head
    kv_local = key_rows.shape[2] // D_HEAD // n_head
    q_local = queries.shape[2] // D_HEAD // n_head
    groups = q_local // kv_local
    query_flat = ctx_index * seg_rows + jnp.arange(seg_rows, dtype=jnp.int32)
    query_pos = lookup_positions(stretch_order, query_flat, span)
    initial = (
        jnp.full((kv_local, groups, seg_rows), NEG_FILL, jnp.float32),
        jnp.zeros((kv_local, groups, seg_rows), jnp.float32),
        jnp.zeros((kv_local, groups, seg_rows, D_HEAD), jnp.float32),
    )
    query_ex, key_ex, value_ex = (
        lax.all_to_all(queries, "head", split_axis=2, concat_axis=1, tiled=True),
        lax.all_to_all(key_rows, "head", split_axis=2, concat_axis=1, tiled=True),
        lax.all_to_all(value_rows, "head", split_axis=2, concat_axis=1, tiled=True),
    )
    query_heads = query_ex[0].reshape(seg_rows, kv_local, groups, D_HEAD)
    keys = lax.all_gather(key_ex[0], "ctx", axis=0, tiled=True)
    values = lax.all_gather(value_ex[0], "ctx", axis=0, tiled=True)
    flat_rows = jnp.arange(keys.shape[0], dtype=jnp.int32)
    final = fold_piece(
        initial, query_heads, query_pos, keys, values, flat_rows, stretch_order, span, kv_local
    )
    run_max, run_sum, run_acc = final
    mixed = run_acc / run_sum[..., None]
    attn = (
        jnp.transpose(mixed, (2, 0, 1, 3)).reshape(seg_rows, q_local * D_HEAD).astype(jnp.bfloat16)
    )
    partial_out = jnp.dot(attn, out_weight, preferred_element_type=jnp.float32).astype(jnp.bfloat16)
    return (
        lax.psum_scatter(partial_out, "head", scatter_dimension=1, tiled=True)
        .astype(jnp.float32)
        .astype(jnp.bfloat16)
    )


def solution(mesh):
    n_head, n_ctx = mesh.shape["head"], mesh.shape["ctx"]

    def on_device(*args):
        if n_ctx <= 8:
            return fast_path(*args, n_head, n_ctx)
        return long_path(*args, n_head)

    return jax.shard_map(
        on_device,
        mesh=mesh,
        in_specs=(
            P("ctx", "head", None),
            P("ctx", "head", None),
            P("ctx", "head", None),
            P(),
            P("head", None),
        ),
        out_specs=P("ctx", "head"),
        check_vma=False,
    )
```

```python
import functools
import math

import jax
import jax.numpy as jnp
from jax import lax
from jax.experimental import pallas as pl
from jax.experimental.pallas import tpu as pltpu
from jax.sharding import PartitionSpec as P

D_HEAD = 128
NEG_FILL = -1e30
ROOMY = 42
STRIPE = 256
FETCHES = 8
PARTS = 2
EXP2_SCALE = D_HEAD ** (-0.5) * math.log2(math.e)


def swap(x, axis, flip, size):
    return lax.ppermute(x, axis, [(i, i ^ flip) for i in range(size)])


def swap_by_core(x, flips, n_head, n_ctx):
    pairs = [
        (j * n_ctx + c, (j ^ flips[c % 2]) * n_ctx + c) for j in range(n_head) for c in range(n_ctx)
    ]
    return lax.ppermute(x, ("head", "ctx"), pairs)


def first_flip():
    return 1 + lax.rem(lax.axis_index("ctx"), 2)


def lookup_positions(order, flat_rows, span):
    table = jnp.arange(order.shape[0], dtype=jnp.int32)
    hits = (flat_rows // span)[:, None] == table[None, :]
    return jnp.sum(jnp.where(hits, order[None, :], 0), axis=1) * span + flat_rows % span


def prepare_kernel(span, n_head, chunk_flips, order_hbm, weight_ref, after_ref, *refs):
    weight_out, qpos_ref, kpos_ref, sems, order_ref, order_sem = refs[-6:]
    order_copy = pltpu.make_async_copy(order_hbm, order_ref, order_sem)
    order_copy.start()
    me, ctx = lax.axis_index("head"), lax.axis_index("ctx")
    step = weight_ref.shape[0] // FETCHES
    fetches = [
        pltpu.make_async_copy(
            weight_ref.at[i * step : (i + 1) * step], weight_out.at[i * step : (i + 1) * step], sems.at[i]
        )
        for i in range(FETCHES)
    ]

    @pl.when(me >= 0)
    def start():
        for fetch in fetches:
            fetch.start()

    order_copy.wait()
    row = lax.broadcasted_iota(jnp.int32, (span, D_HEAD), 0)
    for i, flip in enumerate(chunk_flips):
        for k in range(n_head):
            first = (i * n_head + k) * span
            block = order_ref[(ctx ^ flip) * n_head + (me ^ k)]
            kpos_ref[first : first + span, :] = row + block * span
    heads = qpos_ref.shape[1] // (span * n_head)
    lane = lax.broadcasted_iota(jnp.int32, qpos_ref.shape, 1)
    qpos = lane
    for i in range(heads * n_head):
        block = order_ref[ctx * n_head + i % n_head]
        qpos = jnp.where(lane >= i * span, lane + (block - i) * span, qpos)
    qpos_ref[...] = qpos
    for fetch in fetches:
        fetch.wait()


def prepare(order, weight, after, q_pieces, others, chunk_flips, n_keys):
    n_head = len(q_pieces)
    span, width = q_pieces[0].shape
    columns = span * n_head * width // D_HEAD
    n_order = order.shape[0]
    vmem = pl.BlockSpec(memory_space=pltpu.VMEM)
    return pl.pallas_call(
        functools.partial(prepare_kernel, span, n_head, chunk_flips),
        out_shape=(
            jax.ShapeDtypeStruct(weight.shape, weight.dtype),
            jax.ShapeDtypeStruct((1, columns), jnp.int32),
            jax.ShapeDtypeStruct((n_keys, D_HEAD), jnp.int32),
        ),
        in_specs=[
            pl.BlockSpec(memory_space=pltpu.HBM),
            pl.BlockSpec(memory_space=pltpu.HBM),
            pl.BlockSpec(memory_space=pl.ANY),
        ]
        + [pl.BlockSpec(memory_space=pl.ANY)] * len(others),
        out_specs=(vmem,) * 3,
        scratch_shapes=[
            pltpu.SemaphoreType.DMA((FETCHES,)),
            pltpu.SMEM((n_order,), jnp.int32),
            pltpu.SemaphoreType.DMA(()),
        ],
        compiler_params=pltpu.CompilerParams(vmem_limit_bytes=ROOMY * 1024 * 1024),
        cost_estimate=pl.CostEstimate(flops=0, bytes_accessed=4 * 1024 * 1024, transcendentals=0),
    )(order, weight, after, *others)


def assemble_kernel(*refs):
    q_refs, (q_out, q_s) = refs[:-2], refs[-2:]
    me = lax.axis_index("head")
    span, width = q_refs[0].shape
    for k, q_ref in enumerate(q_refs):
        at = pl.multiple_of((me ^ k) * span, span)
        q_s[pl.ds(at, span), :] = q_ref[...].astype(jnp.float32)
    heads = range(width // D_HEAD)
    stacked = jnp.concatenate([q_s[:, h * D_HEAD : (h + 1) * D_HEAD] for h in heads], axis=0)
    q_out[...] = stacked.T.astype(jnp.bfloat16)


def assemble(q_pieces):
    n_head = len(q_pieces)
    span, width = q_pieces[0].shape
    seg = span * n_head
    vmem = pl.BlockSpec(memory_space=pltpu.VMEM)
    return pl.pallas_call(
        assemble_kernel,
        out_shape=jax.ShapeDtypeStruct((D_HEAD, seg * width // D_HEAD), jnp.bfloat16),
        in_specs=[vmem] * n_head,
        out_specs=vmem,
        scratch_shapes=[pltpu.VMEM((seg, width), jnp.float32)],
        compiler_params=pltpu.CompilerParams(vmem_limit_bytes=8 * 1024 * 1024),
        cost_estimate=pl.CostEstimate(flops=0, bytes_accessed=1024 * 1024, transcendentals=0),
    )(*q_pieces)


def project(attn, weight_ref, flip, cols):
    at = pl.multiple_of((lax.axis_index("head") ^ flip) * cols, cols)
    part = jnp.dot(attn, weight_ref[:, pl.ds(at, cols)], preferred_element_type=jnp.float32)
    return part.astype(jnp.bfloat16)


def fold_keys(kv_refs, kpos, qpos_ref, q_ref, state, emit):
    keys = jnp.concatenate([ref[:, :D_HEAD] for ref in kv_refs], axis=0)
    values = jnp.concatenate([ref[:, D_HEAD:] for ref in kv_refs], axis=0).T
    kpos = jnp.concatenate([kpos] * (STRIPE // D_HEAD), axis=1)

    def score(at):
        scores = jnp.dot(keys, q_ref[:, at], preferred_element_type=jnp.float32)
        return jnp.where(kpos <= qpos_ref[:, at], scores, NEG_FILL)

    def weigh(at, scores):
        peak = jnp.max(scores, axis=0, keepdims=True)
        if state is not None:
            peak = jnp.maximum(state[0][:, at], peak)
        weights = jnp.exp2((scores - peak) * EXP2_SCALE)
        return peak, jnp.sum(weights, axis=0, keepdims=True), weights.astype(jnp.bfloat16)

    def finish(at, peak, denom, weights):
        mixed = jnp.dot(values, weights, preferred_element_type=jnp.float32)
        if state is not None:
            factor = jnp.exp2((state[0][:, at] - peak) * EXP2_SCALE)
            denom = factor * state[1][:, at] + denom
            mixed = factor * state[2][:, at] + mixed
        emit(at, peak, denom, mixed)

    stripes = [slice(i, i + STRIPE) for i in range(0, q_ref.shape[1], STRIPE)]
    scores, held = score(stripes[0]), None
    for i, at in enumerate(stripes):
        ahead = score(stripes[i + 1]) if i + 1 < len(stripes) else None
        weighed = weigh(at, scores)
        if held is not None:
            finish(stripes[i - 1], *held)
        scores, held = ahead, weighed
    finish(stripes[-1], *held)


def early_kernel(n_chunk, kpos_ref, qpos_ref, q_ref, *refs):
    kv_refs, out = refs[:n_chunk], refs[n_chunk:]
    n_keys = sum(ref.shape[0] for ref in kv_refs)

    def emit(at, peak, denom, mixed):
        for ref, value in zip(out, (peak, denom, mixed), strict=True):
            ref[:, at] = value

    fold_keys(kv_refs, kpos_ref[:n_keys, :], qpos_ref, q_ref, None, emit)


def early_attend(kpos, qpos, q_all, kv_chunks):
    n_chunk, (depth, columns) = len(kv_chunks), q_all.shape
    n_keys = sum(chunk.shape[0] for chunk in kv_chunks)
    vmem = pl.BlockSpec(memory_space=pltpu.VMEM)
    line = jax.ShapeDtypeStruct((1, columns), jnp.float32)
    return pl.pallas_call(
        functools.partial(early_kernel, n_chunk),
        out_shape=(line, line, jax.ShapeDtypeStruct((depth, columns), jnp.float32)),
        in_specs=[vmem] * (3 + n_chunk),
        out_specs=(vmem,) * 3,
        compiler_params=pltpu.CompilerParams(vmem_limit_bytes=20 * 1024 * 1024),
        cost_estimate=pl.CostEstimate(
            flops=4 * columns * depth * n_keys,
            bytes_accessed=4 * 1024 * 1024,
            transcendentals=columns * n_keys,
        ),
    )(kpos, qpos, q_all, *kv_chunks)


def attend_kernel(n_chunk, kpos_ref, qpos_ref, q_ref, *refs):
    kv_refs, state = refs[:n_chunk], refs[n_chunk : n_chunk + 3]
    weight_ref, attn_ref, *far_refs = refs[n_chunk + 3 :]
    seg, width = attn_ref.shape
    n_keys = sum(ref.shape[0] for ref in kv_refs)
    rows = []

    def emit(at, peak, denom, mixed):
        rows.append((mixed * (1.0 / denom)).T.astype(jnp.bfloat16))

    fold_keys(kv_refs, kpos_ref[n_keys:, :], qpos_ref, q_ref, state, emit)
    rows = jnp.concatenate(rows, axis=0)
    heads = width // D_HEAD
    attn = jnp.concatenate([rows[h * seg : (h + 1) * seg] for h in range(heads)], axis=1)
    attn_ref[...] = attn
    split_rows(project(attn, weight_ref, 3, far_refs[0].shape[1]), far_refs)


def attend(kpos, qpos, q_all, kv_chunks, state, weight, n_head):
    n_chunk, (depth, columns) = len(kv_chunks), q_all.shape
    width, out_width = weight.shape
    seg = columns * depth // width
    n_keys = sum(chunk.shape[0] for chunk in kv_chunks)
    cols = out_width // n_head
    vmem = pl.BlockSpec(memory_space=pltpu.VMEM)
    return pl.pallas_call(
        functools.partial(attend_kernel, n_chunk),
        out_shape=(
            jax.ShapeDtypeStruct((seg, width), jnp.bfloat16),
            *(jax.ShapeDtypeStruct((seg // PARTS, cols), jnp.bfloat16),) * PARTS,
        ),
        in_specs=[vmem] * (7 + n_chunk),
        out_specs=(vmem,) * (1 + PARTS),
        compiler_params=pltpu.CompilerParams(vmem_limit_bytes=28 * 1024 * 1024),
        cost_estimate=pl.CostEstimate(
            flops=4 * columns * depth * n_keys + 2 * seg * width * cols,
            bytes_accessed=4 * 1024 * 1024,
            transcendentals=columns * n_keys,
        ),
    )(kpos, qpos, q_all, *kv_chunks, *state, weight)


def split_rows(block, refs):
    rows = refs[0].shape[0]
    for i, ref in enumerate(refs):
        ref[...] = block[i * rows : (i + 1) * rows]


def near_kernel(attn_ref, weight_ref, first_ref, *second_refs):
    flip, cols = first_flip(), first_ref.shape[1]
    first_ref[...] = project(attn_ref[...], weight_ref, flip, cols)
    split_rows(project(attn_ref[...], weight_ref, 3 - flip, cols), second_refs)


def own_kernel(attn_ref, weight_ref, out_ref):
    out_ref[...] = project(attn_ref[...], weight_ref, 0, out_ref.shape[1])


def project_rest(kernel, out_rows, attn, weight, n_head):
    seg, width = attn.shape
    cols = weight.shape[1] // n_head
    vmem = pl.BlockSpec(memory_space=pltpu.VMEM)
    return pl.pallas_call(
        kernel,
        out_shape=tuple(jax.ShapeDtypeStruct((rows, cols), jnp.bfloat16) for rows in out_rows),
        in_specs=[vmem, vmem],
        out_specs=(vmem,) * len(out_rows),
        compiler_params=pltpu.CompilerParams(vmem_limit_bytes=20 * 1024 * 1024),
        cost_estimate=pl.CostEstimate(
            flops=2 * sum(out_rows) * width * cols,
            bytes_accessed=2 * width * cols,
            transcendentals=0,
        ),
    )(attn, weight)


def sum_kernel(mine_ref, theirs_ref, out_ref):
    total = mine_ref[...].astype(jnp.float32) + theirs_ref[...].astype(jnp.float32)
    out_ref[...] = total.astype(jnp.bfloat16)


def final_kernel(kept_ref, received_ref, *refs):
    out_ref = refs[-1]
    rows = refs[0].shape[0]
    for i, ref in enumerate(refs[:-1]):
        at = slice(i * rows, (i + 1) * rows)
        total = kept_ref[at].astype(jnp.float32) + received_ref[at].astype(jnp.float32)
        out_ref[at] = (total + ref[...].astype(jnp.float32)).astype(jnp.bfloat16)


def sum_blocks(kernel, *blocks):
    vmem = pl.BlockSpec(memory_space=pltpu.VMEM)
    size = blocks[0].size * len(blocks)
    return pl.pallas_call(
        kernel,
        out_shape=jax.ShapeDtypeStruct(blocks[0].shape, jnp.bfloat16),
        in_specs=[vmem] * len(blocks),
        out_specs=vmem,
        compiler_params=pltpu.CompilerParams(vmem_limit_bytes=6 * 1024 * 1024),
        cost_estimate=pl.CostEstimate(flops=size, bytes_accessed=2 * size, transcendentals=0),
    )(*blocks)


def fast_path(queries, key_rows, value_rows, stretch_order, out_weight, n_head, n_ctx):
    me = lax.axis_index("head")

    def cut(x, k):
        width = x.shape[2] // n_head
        return lax.dynamic_slice_in_dim(x[0], (me ^ k) * width, width, 1)

    kv_cut = [
        jnp.concatenate([cut(key_rows, k), cut(value_rows, k)], axis=1) for k in range(n_head)
    ]
    q_cut = [cut(queries, k) for k in range(n_head)]
    kv_in = [kv_cut[0]] + [swap(kv_cut[k], "head", k, n_head) for k in range(1, n_head)]
    own = jnp.concatenate(kv_in, axis=0)
    q_in = [q_cut[0]] + [swap(q_cut[k], "head", k, n_head) for k in range(1, n_head)]
    flips = [2 * dz for dz in range(n_ctx // 2)]
    seg = own.shape[0]
    chunk_flips = tuple(flips + [f ^ 1 for f in flips])
    q_all = assemble(q_in)
    weight, qpos, kpos = prepare(
        stretch_order, out_weight, own, q_in, [q_in[k] for k in (2, 3)], chunk_flips, own.shape[0] * n_ctx
    )
    far_keys = [swap(own, "ctx", f, n_ctx) for f in flips[1:]]
    far_keys, kpos = lax.optimization_barrier((far_keys, kpos))
    same_core = [own] + far_keys
    other_core = [swap(x, "ctx", 1, n_ctx) for x in (own, *far_keys)]
    state = early_attend(kpos, qpos, q_all, same_core)
    attn, *far = attend(kpos, qpos, q_all, other_core, state, weight, n_head)
    passed = [swap_by_core(x, (1, 2), n_head, n_ctx) for x in far]
    half = seg // PARTS
    first, *second = project_rest(near_kernel, (seg,) + (half,) * PARTS, attn, weight, n_head)
    received = swap_by_core(first, (1, 2), n_head, n_ctx)
    (kept,) = project_rest(own_kernel, (seg,), attn, weight, n_head)
    joined = [
        swap_by_core(sum_blocks(sum_kernel, mine, theirs), (2, 1), n_head, n_ctx)
        for mine, theirs in zip(second, passed, strict=True)
    ]
    return sum_blocks(final_kernel, kept, received, *joined)


def attend_block(state, query_heads, query_pos, key_block, value_block, key_pos):
    run_max, run_sum, run_acc = state
    scores = jnp.einsum(
        "tkgd,pkd->kgtp", query_heads, key_block, preferred_element_type=jnp.float32
    ) * D_HEAD ** (-0.5)
    visible = key_pos[None, :] <= query_pos[:, None]
    scores = jnp.where(visible, scores, NEG_FILL)
    new_max = jnp.maximum(run_max, jnp.max(scores, axis=3))
    weights = jnp.where(visible, jnp.exp(scores - new_max[..., None]), 0.0)
    factor = jnp.exp(run_max - new_max)
    new_sum = run_sum * factor + jnp.sum(weights, axis=3)
    product = jnp.einsum(
        "kgtp,pkd->kgtd",
        weights.astype(jnp.bfloat16),
        value_block,
        preferred_element_type=jnp.float32,
    )
    return (new_max, new_sum, run_acc * factor[..., None] + product)


def fold_piece(
    state, query_heads, query_pos, key_piece, value_piece, flat_rows, order, span, kv_heads
):
    count = key_piece.shape[0]
    width = 512 if count % 512 == 0 else count
    blocks_n = count // width
    key_blocks = key_piece.reshape(blocks_n, width, kv_heads, D_HEAD)
    value_blocks = value_piece.reshape(blocks_n, width, kv_heads, D_HEAD)
    flat_blocks = flat_rows.reshape(blocks_n, width)

    def step_block(current, slab):
        key_block, value_block, block_rows = slab
        key_pos = lookup_positions(order, block_rows, span)
        return (
            attend_block(current, query_heads, query_pos, key_block, value_block, key_pos),
            None,
        )

    state, unused = lax.scan(step_block, state, (key_blocks, value_blocks, flat_blocks))
    return state


def long_path(queries, key_rows, value_rows, stretch_order, out_weight, n_head):
    ctx_index = lax.axis_index("ctx")
    span = queries.shape[1]
    seg_rows = span * n_head
    kv_local = key_rows.shape[2] // D_HEAD // n_head
    q_local = queries.shape[2] // D_HEAD // n_head
    groups = q_local // kv_local
    query_flat = ctx_index * seg_rows + jnp.arange(seg_rows, dtype=jnp.int32)
    query_pos = lookup_positions(stretch_order, query_flat, span)
    initial = (
        jnp.full((kv_local, groups, seg_rows), NEG_FILL, jnp.float32),
        jnp.zeros((kv_local, groups, seg_rows), jnp.float32),
        jnp.zeros((kv_local, groups, seg_rows, D_HEAD), jnp.float32),
    )
    query_ex, key_ex, value_ex = (
        lax.all_to_all(queries, "head", split_axis=2, concat_axis=1, tiled=True),
        lax.all_to_all(key_rows, "head", split_axis=2, concat_axis=1, tiled=True),
        lax.all_to_all(value_rows, "head", split_axis=2, concat_axis=1, tiled=True),
    )
    query_heads = query_ex[0].reshape(seg_rows, kv_local, groups, D_HEAD)
    keys = lax.all_gather(key_ex[0], "ctx", axis=0, tiled=True)
    values = lax.all_gather(value_ex[0], "ctx", axis=0, tiled=True)
    flat_rows = jnp.arange(keys.shape[0], dtype=jnp.int32)
    final = fold_piece(
        initial, query_heads, query_pos, keys, values, flat_rows, stretch_order, span, kv_local
    )
    run_max, run_sum, run_acc = final
    mixed = run_acc / run_sum[..., None]
    attn = (
        jnp.transpose(mixed, (2, 0, 1, 3)).reshape(seg_rows, q_local * D_HEAD).astype(jnp.bfloat16)
    )
    partial_out = jnp.dot(attn, out_weight, preferred_element_type=jnp.float32).astype(jnp.bfloat16)
    return (
        lax.psum_scatter(partial_out, "head", scatter_dimension=1, tiled=True)
        .astype(jnp.float32)
        .astype(jnp.bfloat16)
    )


def solution(mesh):
    n_head, n_ctx = mesh.shape["head"], mesh.shape["ctx"]

    def on_device(*args):
        if n_ctx <= 8:
            return fast_path(*args, n_head, n_ctx)
        return long_path(*args, n_head)

    return jax.shard_map(
        on_device,
        mesh=mesh,
        in_specs=(
            P("ctx", "head", None),
            P("ctx", "head", None),
            P("ctx", "head", None),
            P(),
            P("head", None),
        ),
        out_specs=P("ctx", "head"),
        check_vma=False,
    )
```

```python
import functools
import math

import jax
import jax.numpy as jnp
from jax import lax
from jax.experimental import pallas as pl
from jax.experimental.pallas import tpu as pltpu
from jax.sharding import PartitionSpec as P

D_HEAD = 128
NEG_FILL = -1e30
ROOMY = 42
STRIPE = 256
SUM_ROWS = 16
FETCHES = 8
PARTS = 2
EXP2_SCALE = D_HEAD ** (-0.5) * math.log2(math.e)


def swap(x, axis, flip, size):
    return lax.ppermute(x, axis, [(i, i ^ flip) for i in range(size)])


def swap_by_core(x, flips, n_head, n_ctx):
    pairs = [
        (j * n_ctx + c, (j ^ flips[c % 2]) * n_ctx + c) for j in range(n_head) for c in range(n_ctx)
    ]
    return lax.ppermute(x, ("head", "ctx"), pairs)


def first_flip():
    return 1 + lax.rem(lax.axis_index("ctx"), 2)


def lookup_positions(order, flat_rows, span):
    table = jnp.arange(order.shape[0], dtype=jnp.int32)
    hits = (flat_rows // span)[:, None] == table[None, :]
    return jnp.sum(jnp.where(hits, order[None, :], 0), axis=1) * span + flat_rows % span


def prepare_kernel(span, n_head, chunk_flips, order_hbm, weight_ref, after_ref, *refs):
    weight_out, qpos_ref, kpos_ref, sems, order_ref, order_sem = refs[-6:]
    order_copy = pltpu.make_async_copy(order_hbm, order_ref, order_sem)
    order_copy.start()
    me, ctx = lax.axis_index("head"), lax.axis_index("ctx")
    step = weight_ref.shape[0] // FETCHES
    fetches = [
        pltpu.make_async_copy(
            weight_ref.at[i * step : (i + 1) * step], weight_out.at[i * step : (i + 1) * step], sems.at[i]
        )
        for i in range(FETCHES)
    ]

    @pl.when(me >= 0)
    def start():
        for fetch in fetches:
            fetch.start()

    order_copy.wait()
    row = lax.broadcasted_iota(jnp.int32, (span, D_HEAD), 0)
    for i, flip in enumerate(chunk_flips):
        for k in range(n_head):
            first = (i * n_head + k) * span
            block = order_ref[(ctx ^ flip) * n_head + (me ^ k)]
            kpos_ref[first : first + span, :] = row + block * span
    heads = qpos_ref.shape[1] // (span * n_head)
    lane = lax.broadcasted_iota(jnp.int32, qpos_ref.shape, 1)
    qpos = lane
    for i in range(heads * n_head):
        block = order_ref[ctx * n_head + i % n_head]
        qpos = jnp.where(lane >= i * span, lane + (block - i) * span, qpos)
    qpos_ref[...] = qpos
    for fetch in fetches:
        fetch.wait()


def prepare(order, weight, after, q_pieces, others, chunk_flips, n_keys):
    n_head = len(q_pieces)
    span, width = q_pieces[0].shape
    columns = span * n_head * width // D_HEAD
    n_order = order.shape[0]
    vmem = pl.BlockSpec(memory_space=pltpu.VMEM)
    return pl.pallas_call(
        functools.partial(prepare_kernel, span, n_head, chunk_flips),
        out_shape=(
            jax.ShapeDtypeStruct(weight.shape, weight.dtype),
            jax.ShapeDtypeStruct((1, columns), jnp.int32),
            jax.ShapeDtypeStruct((n_keys, D_HEAD), jnp.int32),
        ),
        in_specs=[
            pl.BlockSpec(memory_space=pltpu.HBM),
            pl.BlockSpec(memory_space=pltpu.HBM),
            pl.BlockSpec(memory_space=pl.ANY),
        ]
        + [pl.BlockSpec(memory_space=pl.ANY)] * len(others),
        out_specs=(vmem,) * 3,
        scratch_shapes=[
            pltpu.SemaphoreType.DMA((FETCHES,)),
            pltpu.SMEM((n_order,), jnp.int32),
            pltpu.SemaphoreType.DMA(()),
        ],
        compiler_params=pltpu.CompilerParams(vmem_limit_bytes=ROOMY * 1024 * 1024),
        cost_estimate=pl.CostEstimate(flops=0, bytes_accessed=4 * 1024 * 1024, transcendentals=0),
    )(order, weight, after, *others)


def assemble_kernel(*refs):
    q_refs, (q_out, q_s) = refs[:-2], refs[-2:]
    me = lax.axis_index("head")
    span, width = q_refs[0].shape
    for k, q_ref in enumerate(q_refs):
        at = pl.multiple_of((me ^ k) * span, span)
        q_s[pl.ds(at, span), :] = q_ref[...].astype(jnp.float32)
    heads = range(width // D_HEAD)
    stacked = jnp.concatenate([q_s[:, h * D_HEAD : (h + 1) * D_HEAD] for h in heads], axis=0)
    q_out[...] = stacked.T.astype(jnp.bfloat16)


def assemble(q_pieces):
    n_head = len(q_pieces)
    span, width = q_pieces[0].shape
    seg = span * n_head
    vmem = pl.BlockSpec(memory_space=pltpu.VMEM)
    return pl.pallas_call(
        assemble_kernel,
        out_shape=jax.ShapeDtypeStruct((D_HEAD, seg * width // D_HEAD), jnp.bfloat16),
        in_specs=[vmem] * n_head,
        out_specs=vmem,
        scratch_shapes=[pltpu.VMEM((seg, width), jnp.float32)],
        compiler_params=pltpu.CompilerParams(vmem_limit_bytes=8 * 1024 * 1024),
        cost_estimate=pl.CostEstimate(flops=0, bytes_accessed=1024 * 1024, transcendentals=0),
    )(*q_pieces)


def project(attn, weight_ref, flip, cols):
    at = pl.multiple_of((lax.axis_index("head") ^ flip) * cols, cols)
    part = jnp.dot(attn, weight_ref[:, pl.ds(at, cols)], preferred_element_type=jnp.float32)
    return part.astype(jnp.bfloat16)


def fold_keys(kv_refs, kpos, qpos_ref, q_ref, state, emit):
    keys = jnp.concatenate([ref[:, :D_HEAD] for ref in kv_refs], axis=0)
    values = jnp.concatenate([ref[:, D_HEAD:] for ref in kv_refs], axis=0).T
    ones = jnp.ones((SUM_ROWS, values.shape[1]), values.dtype)
    values = jnp.concatenate([values, ones], axis=0)
    kpos = jnp.concatenate([kpos] * (STRIPE // D_HEAD), axis=1)

    def score(at):
        scores = jnp.dot(keys, q_ref[:, at], preferred_element_type=jnp.float32)
        return jnp.where(kpos <= qpos_ref[:, at], scores, NEG_FILL)

    def weigh(at, scores):
        peak = jnp.max(scores, axis=0, keepdims=True)
        if state is not None:
            peak = jnp.maximum(state[0][:, at], peak)
        weights = jnp.exp2((scores - peak) * EXP2_SCALE)
        return peak, weights.astype(jnp.bfloat16)

    def finish(at, peak, weights):
        product = jnp.dot(values, weights, preferred_element_type=jnp.float32)
        mixed, denom = product[:D_HEAD], product[D_HEAD : D_HEAD + 1]
        if state is not None:
            factor = jnp.exp2((state[0][:, at] - peak) * EXP2_SCALE)
            denom = factor * state[1][:, at] + denom
            mixed = factor * state[2][:, at] + mixed
        emit(at, peak, denom, mixed)

    stripes = [slice(i, i + STRIPE) for i in range(0, q_ref.shape[1], STRIPE)]
    scores, held = score(stripes[0]), None
    for i, at in enumerate(stripes):
        ahead = score(stripes[i + 1]) if i + 1 < len(stripes) else None
        weighed = weigh(at, scores)
        if held is not None:
            finish(stripes[i - 1], *held)
        scores, held = ahead, weighed
    finish(stripes[-1], *held)


def early_kernel(n_chunk, kpos_ref, qpos_ref, q_ref, *refs):
    kv_refs, out = refs[:n_chunk], refs[n_chunk:]
    n_keys = sum(ref.shape[0] for ref in kv_refs)

    def emit(at, peak, denom, mixed):
        for ref, value in zip(out, (peak, denom, mixed), strict=True):
            ref[:, at] = value

    fold_keys(kv_refs, kpos_ref[:n_keys, :], qpos_ref, q_ref, None, emit)


def early_attend(kpos, qpos, q_all, kv_chunks):
    n_chunk, (depth, columns) = len(kv_chunks), q_all.shape
    n_keys = sum(chunk.shape[0] for chunk in kv_chunks)
    vmem = pl.BlockSpec(memory_space=pltpu.VMEM)
    line = jax.ShapeDtypeStruct((1, columns), jnp.float32)
    return pl.pallas_call(
        functools.partial(early_kernel, n_chunk),
        out_shape=(line, line, jax.ShapeDtypeStruct((depth, columns), jnp.float32)),
        in_specs=[vmem] * (3 + n_chunk),
        out_specs=(vmem,) * 3,
        compiler_params=pltpu.CompilerParams(vmem_limit_bytes=20 * 1024 * 1024),
        cost_estimate=pl.CostEstimate(
            flops=4 * columns * depth * n_keys,
            bytes_accessed=4 * 1024 * 1024,
            transcendentals=columns * n_keys,
        ),
    )(kpos, qpos, q_all, *kv_chunks)


def attend_kernel(n_chunk, kpos_ref, qpos_ref, q_ref, *refs):
    kv_refs, state = refs[:n_chunk], refs[n_chunk : n_chunk + 3]
    weight_ref, attn_ref, *far_refs = refs[n_chunk + 3 :]
    seg, width = attn_ref.shape
    n_keys = sum(ref.shape[0] for ref in kv_refs)
    rows = []

    def emit(at, peak, denom, mixed):
        rows.append((mixed * (1.0 / denom)).T.astype(jnp.bfloat16))

    fold_keys(kv_refs, kpos_ref[n_keys:, :], qpos_ref, q_ref, state, emit)
    rows = jnp.concatenate(rows, axis=0)
    heads = width // D_HEAD
    attn = jnp.concatenate([rows[h * seg : (h + 1) * seg] for h in range(heads)], axis=1)
    attn_ref[...] = attn
    split_rows(project(attn, weight_ref, 3, far_refs[0].shape[1]), far_refs)


def attend(kpos, qpos, q_all, kv_chunks, state, weight, n_head):
    n_chunk, (depth, columns) = len(kv_chunks), q_all.shape
    width, out_width = weight.shape
    seg = columns * depth // width
    n_keys = sum(chunk.shape[0] for chunk in kv_chunks)
    cols = out_width // n_head
    vmem = pl.BlockSpec(memory_space=pltpu.VMEM)
    return pl.pallas_call(
        functools.partial(attend_kernel, n_chunk),
        out_shape=(
            jax.ShapeDtypeStruct((seg, width), jnp.bfloat16),
            *(jax.ShapeDtypeStruct((seg // PARTS, cols), jnp.bfloat16),) * PARTS,
        ),
        in_specs=[vmem] * (7 + n_chunk),
        out_specs=(vmem,) * (1 + PARTS),
        compiler_params=pltpu.CompilerParams(vmem_limit_bytes=28 * 1024 * 1024),
        cost_estimate=pl.CostEstimate(
            flops=4 * columns * depth * n_keys + 2 * seg * width * cols,
            bytes_accessed=4 * 1024 * 1024,
            transcendentals=columns * n_keys,
        ),
    )(kpos, qpos, q_all, *kv_chunks, *state, weight)


def split_rows(block, refs):
    rows = refs[0].shape[0]
    for i, ref in enumerate(refs):
        ref[...] = block[i * rows : (i + 1) * rows]


def near_kernel(attn_ref, weight_ref, first_ref, *second_refs):
    flip, cols = first_flip(), first_ref.shape[1]
    first_ref[...] = project(attn_ref[...], weight_ref, flip, cols)
    split_rows(project(attn_ref[...], weight_ref, 3 - flip, cols), second_refs)


def own_kernel(attn_ref, weight_ref, out_ref):
    out_ref[...] = project(attn_ref[...], weight_ref, 0, out_ref.shape[1])


def project_rest(kernel, out_rows, attn, weight, n_head):
    seg, width = attn.shape
    cols = weight.shape[1] // n_head
    vmem = pl.BlockSpec(memory_space=pltpu.VMEM)
    return pl.pallas_call(
        kernel,
        out_shape=tuple(jax.ShapeDtypeStruct((rows, cols), jnp.bfloat16) for rows in out_rows),
        in_specs=[vmem, vmem],
        out_specs=(vmem,) * len(out_rows),
        compiler_params=pltpu.CompilerParams(vmem_limit_bytes=20 * 1024 * 1024),
        cost_estimate=pl.CostEstimate(
            flops=2 * sum(out_rows) * width * cols,
            bytes_accessed=2 * width * cols,
            transcendentals=0,
        ),
    )(attn, weight)


def sum_kernel(mine_ref, theirs_ref, out_ref):
    total = mine_ref[...].astype(jnp.float32) + theirs_ref[...].astype(jnp.float32)
    out_ref[...] = total.astype(jnp.bfloat16)


def final_kernel(kept_ref, received_ref, *refs):
    out_ref = refs[-1]
    rows = refs[0].shape[0]
    for i, ref in enumerate(refs[:-1]):
        at = slice(i * rows, (i + 1) * rows)
        total = kept_ref[at].astype(jnp.float32) + received_ref[at].astype(jnp.float32)
        out_ref[at] = (total + ref[...].astype(jnp.float32)).astype(jnp.bfloat16)


def sum_blocks(kernel, *blocks):
    vmem = pl.BlockSpec(memory_space=pltpu.VMEM)
    size = blocks[0].size * len(blocks)
    return pl.pallas_call(
        kernel,
        out_shape=jax.ShapeDtypeStruct(blocks[0].shape, jnp.bfloat16),
        in_specs=[vmem] * len(blocks),
        out_specs=vmem,
        compiler_params=pltpu.CompilerParams(vmem_limit_bytes=6 * 1024 * 1024),
        cost_estimate=pl.CostEstimate(flops=size, bytes_accessed=2 * size, transcendentals=0),
    )(*blocks)


def fast_path(queries, key_rows, value_rows, stretch_order, out_weight, n_head, n_ctx):
    me = lax.axis_index("head")

    def cut(x, k):
        width = x.shape[2] // n_head
        return lax.dynamic_slice_in_dim(x[0], (me ^ k) * width, width, 1)

    kv_cut = [
        jnp.concatenate([cut(key_rows, k), cut(value_rows, k)], axis=1) for k in range(n_head)
    ]
    q_cut = [cut(queries, k) for k in range(n_head)]
    kv_in = [kv_cut[0]] + [swap(kv_cut[k], "head", k, n_head) for k in range(1, n_head)]
    own = jnp.concatenate(kv_in, axis=0)
    q_in = [q_cut[0]] + [swap(q_cut[k], "head", k, n_head) for k in range(1, n_head)]
    flips = [2 * dz for dz in range(n_ctx // 2)]
    seg = own.shape[0]
    chunk_flips = tuple(flips + [f ^ 1 for f in flips])
    q_all = assemble(q_in)
    weight, qpos, kpos = prepare(
        stretch_order, out_weight, own, q_in, [q_in[k] for k in (2, 3)], chunk_flips, own.shape[0] * n_ctx
    )
    far_keys = [swap(own, "ctx", f, n_ctx) for f in flips[1:]]
    far_keys, kpos = lax.optimization_barrier((far_keys, kpos))
    same_core = [own] + far_keys
    other_core = [swap(x, "ctx", 1, n_ctx) for x in (own, *far_keys)]
    state = early_attend(kpos, qpos, q_all, same_core)
    attn, *far = attend(kpos, qpos, q_all, other_core, state, weight, n_head)
    passed = [swap_by_core(x, (1, 2), n_head, n_ctx) for x in far]
    half = seg // PARTS
    first, *second = project_rest(near_kernel, (seg,) + (half,) * PARTS, attn, weight, n_head)
    received = swap_by_core(first, (1, 2), n_head, n_ctx)
    (kept,) = project_rest(own_kernel, (seg,), attn, weight, n_head)
    joined = [
        swap_by_core(sum_blocks(sum_kernel, mine, theirs), (2, 1), n_head, n_ctx)
        for mine, theirs in zip(second, passed, strict=True)
    ]
    return sum_blocks(final_kernel, kept, received, *joined)


def attend_block(state, query_heads, query_pos, key_block, value_block, key_pos):
    run_max, run_sum, run_acc = state
    scores = jnp.einsum(
        "tkgd,pkd->kgtp", query_heads, key_block, preferred_element_type=jnp.float32
    ) * D_HEAD ** (-0.5)
    visible = key_pos[None, :] <= query_pos[:, None]
    scores = jnp.where(visible, scores, NEG_FILL)
    new_max = jnp.maximum(run_max, jnp.max(scores, axis=3))
    weights = jnp.where(visible, jnp.exp(scores - new_max[..., None]), 0.0)
    factor = jnp.exp(run_max - new_max)
    new_sum = run_sum * factor + jnp.sum(weights, axis=3)
    product = jnp.einsum(
        "kgtp,pkd->kgtd",
        weights.astype(jnp.bfloat16),
        value_block,
        preferred_element_type=jnp.float32,
    )
    return (new_max, new_sum, run_acc * factor[..., None] + product)


def fold_piece(
    state, query_heads, query_pos, key_piece, value_piece, flat_rows, order, span, kv_heads
):
    count = key_piece.shape[0]
    width = 512 if count % 512 == 0 else count
    blocks_n = count // width
    key_blocks = key_piece.reshape(blocks_n, width, kv_heads, D_HEAD)
    value_blocks = value_piece.reshape(blocks_n, width, kv_heads, D_HEAD)
    flat_blocks = flat_rows.reshape(blocks_n, width)

    def step_block(current, slab):
        key_block, value_block, block_rows = slab
        key_pos = lookup_positions(order, block_rows, span)
        return (
            attend_block(current, query_heads, query_pos, key_block, value_block, key_pos),
            None,
        )

    state, unused = lax.scan(step_block, state, (key_blocks, value_blocks, flat_blocks))
    return state


def long_path(queries, key_rows, value_rows, stretch_order, out_weight, n_head):
    ctx_index = lax.axis_index("ctx")
    span = queries.shape[1]
    seg_rows = span * n_head
    kv_local = key_rows.shape[2] // D_HEAD // n_head
    q_local = queries.shape[2] // D_HEAD // n_head
    groups = q_local // kv_local
    query_flat = ctx_index * seg_rows + jnp.arange(seg_rows, dtype=jnp.int32)
    query_pos = lookup_positions(stretch_order, query_flat, span)
    initial = (
        jnp.full((kv_local, groups, seg_rows), NEG_FILL, jnp.float32),
        jnp.zeros((kv_local, groups, seg_rows), jnp.float32),
        jnp.zeros((kv_local, groups, seg_rows, D_HEAD), jnp.float32),
    )
    query_ex, key_ex, value_ex = (
        lax.all_to_all(queries, "head", split_axis=2, concat_axis=1, tiled=True),
        lax.all_to_all(key_rows, "head", split_axis=2, concat_axis=1, tiled=True),
        lax.all_to_all(value_rows, "head", split_axis=2, concat_axis=1, tiled=True),
    )
    query_heads = query_ex[0].reshape(seg_rows, kv_local, groups, D_HEAD)
    keys = lax.all_gather(key_ex[0], "ctx", axis=0, tiled=True)
    values = lax.all_gather(value_ex[0], "ctx", axis=0, tiled=True)
    flat_rows = jnp.arange(keys.shape[0], dtype=jnp.int32)
    final = fold_piece(
        initial, query_heads, query_pos, keys, values, flat_rows, stretch_order, span, kv_local
    )
    run_max, run_sum, run_acc = final
    mixed = run_acc / run_sum[..., None]
    attn = (
        jnp.transpose(mixed, (2, 0, 1, 3)).reshape(seg_rows, q_local * D_HEAD).astype(jnp.bfloat16)
    )
    partial_out = jnp.dot(attn, out_weight, preferred_element_type=jnp.float32).astype(jnp.bfloat16)
    return (
        lax.psum_scatter(partial_out, "head", scatter_dimension=1, tiled=True)
        .astype(jnp.float32)
        .astype(jnp.bfloat16)
    )


def solution(mesh):
    n_head, n_ctx = mesh.shape["head"], mesh.shape["ctx"]

    def on_device(*args):
        if n_ctx <= 8:
            return fast_path(*args, n_head, n_ctx)
        return long_path(*args, n_head)

    return jax.shard_map(
        on_device,
        mesh=mesh,
        in_specs=(
            P("ctx", "head", None),
            P("ctx", "head", None),
            P("ctx", "head", None),
            P(),
            P("head", None),
        ),
        out_specs=P("ctx", "head"),
        check_vma=False,
    )
```
